32 devices in a mesh: grp: 1, node: 32 (over z, y, x, core).
Axes of the slice: x: 2, y: 2, z: 4, core: 2. Of those that a mesh axis runs over, the one named last changes fastest.
Arguments:
- hidden_in: bfloat16 [256, 7168], P(('grp', 'node')), may hold values from -6 to 6
- expert_ids: int32 [256, 4], P(('grp', 'node')), may hold values from 0 to 5, all different within a row
- gate_weights: float32 [256, 4], P(('grp', 'node')), may hold values from 0.2 to 1
- replica_pick: int32 [256, 4], P(('grp', 'node')), may hold values from 0 to 7
- placement: int32 [8], replicated, may hold values from 0 to 5, as said below
- capacity: int32 [8], replicated, may hold values from 2 to 4, as said below
- w_gate: bfloat16 [7168, 8192], P(None, 'node'), as said below
- w_up: bfloat16 [7168, 8192], P(None, 'node'), as said below
- w_down: bfloat16 [8192, 7168], P('node'), as said below
Outputs:
- mixed: bfloat16 [256, 7168], P(('grp', 'node'))
The draws below stay inside these ranges and needn't reach their ends.
Inputs may be any that keep to these rules, and one draw needn't show every extreme that they name: `expert_ids`: each row names 4 different experts. `placement`: every expert is hosted by one slot or more. Some slot has capacity 4. `w_gate`: columns s * 1024 to (s + 1) * 1024 - 1 are the gate projection of expert placement[s]; slots that host the same expert hold equal columns. `w_up`: columns s * 1024 to (s + 1) * 1024 - 1 are the up projection of expert placement[s]; slots that host the same expert hold equal columns. `w_down`: rows s * 1024 to (s + 1) * 1024 - 1 are the down projection of expert placement[s]; slots that host the same expert hold equal rows.
All inputs are finite; a program needn't handle non-finite values.
Results may differ from the reference program's by a relative error of at most 0.0058.
Values may be sent and summed in bfloat16 or wider, within the bound.
No kernel may reach another device: no remote copies, remote signals or barrier semaphores. Data moves between devices by JAX's collectives and lax.ppermute only.
A program may use at most 128 MiB of HBM per device.

```python
import jax
import jax.numpy as jnp
from jax import lax

D = 7168
FW = 1024
TOK_DEV = 8
NODES = 8
EXPERTS = 6
TOP = 4
CAP = 4
TOKENS = 256
N_NODE = 32


def placement_of(key):
    first_hosts = jax.random.permutation(jax.random.fold_in(key, 101), EXPERTS)
    extra_hosts = jax.random.randint(jax.random.fold_in(key, 102), (NODES - EXPERTS,), 0, EXPERTS)
    slot_order = jax.random.permutation(jax.random.fold_in(key, 103), NODES)
    return jnp.concatenate([first_hosts, extra_hosts])[slot_order].astype(jnp.int32)


def base_normal(key, shape, spread):
    values = jax.random.normal(key, shape, jnp.float32)
    return values * spread


def draw_placement(key, part):
    return placement_of(key)


def draw_capacity(key, part):
    key = jax.random.fold_in(key, 7)
    lowered = jax.random.randint(jax.random.fold_in(key, 1), (NODES,), CAP // 2, CAP + 1)
    full_slot = jax.random.randint(jax.random.fold_in(key, 2), (), 0, NODES)
    return jnp.where(jnp.arange(NODES) == full_slot, CAP, lowered).astype(jnp.int32)


def draw_w_gate(key, part):
    hosted = placement_of(key)
    key = jax.random.fold_in(key, 11)
    values = base_normal(key, (D, EXPERTS, FW), D ** (-0.5))
    return values[:, hosted, :].reshape(D, NODES * FW).astype(jnp.bfloat16)


def draw_w_up(key, part):
    hosted = placement_of(key)
    key = jax.random.fold_in(key, 12)
    values = base_normal(key, (D, EXPERTS, FW), D ** (-0.5))
    return values[:, hosted, :].reshape(D, NODES * FW).astype(jnp.bfloat16)


def draw_w_down(key, part):
    hosted = placement_of(key)
    key = jax.random.fold_in(key, 13)
    values = base_normal(key, (EXPERTS, FW, D), FW ** (-0.5))
    return values[hosted].reshape(NODES * FW, D).astype(jnp.bfloat16)


def set_ends(drawn, key, least, top_value):
    place = [jax.random.randint(jax.random.fold_in(key, axis), (), 0, length) for axis, length in enumerate(drawn.shape)]
    widest = drawn.shape.index(max(drawn.shape))
    next_to = place[:widest] + [(place[widest] + 1) % drawn.shape[widest]] + place[widest + 1:]
    return drawn.at[tuple(place)].set(least).at[tuple(next_to)].set(top_value)


def block_scale(own_key, dims, cuts, low, top_value):
    gain, own = 1.0, jax.random.fold_in(own_key, 6)
    for dim, shards_of in cuts:
        steps = jnp.exp(jax.random.uniform(jax.random.fold_in(own, dim), (shards_of,), jnp.float32, low / len(cuts), top_value / len(cuts)))
        gain = gain * jnp.repeat(steps, dims[dim] // shards_of).reshape([-1 if axis == dim else 1 for axis in range(len(dims))])
    return gain


def picks_of(own_key, rows, amount, top, lift):
    sequence = jax.random.permutation(jax.random.fold_in(own_key, 1), amount)
    boost = sequence
    for power in range(3):
        boost = boost * boost // amount
    boost = boost * lift // amount
    chance = jax.random.randint(jax.random.fold_in(own_key, 2), (rows, amount), 0, 4096) + boost
    fixed_rows = jax.random.permutation(jax.random.fold_in(own_key, 3), rows)[jnp.arange(amount) % rows]
    chance = jnp.where(jnp.arange(rows)[:, None] == fixed_rows[None, :], 1 << 14, chance)
    merit = chance * amount + jnp.arange(amount)
    return lax.top_k(merit.astype(jnp.int32), top)[1].astype(jnp.int32)


def normal_values(stream_key, extent, scale, limit, pieces=(), kind=jnp.bfloat16):
    result = scale * jax.random.normal(stream_key, extent, jnp.float32)
    if pieces:
        result = result * block_scale(stream_key, extent, pieces, -0.22, 0.18)
    return jnp.clip(result, -limit, limit).astype(kind)


def setup_inputs(seed: int = 0, part: int = 0) -> dict:
    arg_keys = jax.random.split(jax.random.key(seed), 10)
    part_splits = jax.random.split(jax.random.fold_in(arg_keys[9], part), 10)
    hidden_in = normal_values(part_splits[0], (TOKENS, D), 1.0, 6.0, ((0, 32),))
    expert_ids = picks_of(part_splits[1], TOKENS, EXPERTS, TOP, 10922)
    gate_weights = jnp.clip(0.2 + 0.8 * jax.random.uniform(part_splits[2], (TOKENS, TOP), jnp.float32) ** block_scale(part_splits[2], (TOKENS, TOP), ((0, 32),), -0.2, 0.2), 0.2, 1.0)
    replica_pick = set_ends(jax.random.randint(part_splits[3], (TOKENS, TOP), 0, 8), jax.random.fold_in(part_splits[3], 1), 0, 7).astype(jnp.int32)
    placement = draw_placement(jax.random.fold_in(arg_keys[9], 71), part)
    capacity = draw_capacity(jax.random.fold_in(arg_keys[9], 71), part)
    w_gate = draw_w_gate(jax.random.fold_in(arg_keys[9], 71), part)
    w_up = draw_w_up(jax.random.fold_in(arg_keys[9], 71), part)
    w_down = draw_w_down(jax.random.fold_in(arg_keys[9], 71), part)
    return {"hidden_in": hidden_in, "expert_ids": expert_ids, "gate_weights": gate_weights, "replica_pick": replica_pick, "placement": placement, "capacity": capacity, "w_gate": w_gate, "w_up": w_up, "w_down": w_down}


def choose_slots(expert_ids, replica_pick, placement):
    matches = (placement[None, None, :] == expert_ids[:, :, None]).astype(jnp.int32)
    prior_hits = jnp.cumsum(matches, axis=2) - matches
    hosts = jnp.sum(matches, axis=2)
    wanted = replica_pick % hosts
    slot_ids = jnp.arange(placement.shape[0], dtype=jnp.int32)
    chosen = (matches == 1) & (prior_hits == wanted[:, :, None])
    return jnp.sum(jnp.where(chosen, slot_ids[None, None, :], 0), axis=2).astype(jnp.int32)


def rank_in_source(slot_flat, rows_each, slot_count):
    grouped = slot_flat.reshape(-1, rows_each)
    onehot = (grouped[:, :, None] == jnp.arange(slot_count, dtype=jnp.int32)[None, None, :]).astype(jnp.int32)
    earlier = jnp.cumsum(onehot, axis=1) - onehot
    return jnp.sum(onehot * earlier, axis=2).reshape(-1).astype(jnp.int32)


def expert_rows(row_block, gate_cols, up_cols, down_rows):
    gate_act = jnp.dot(row_block, gate_cols, preferred_element_type=jnp.float32)
    up_act = jnp.dot(row_block, up_cols, preferred_element_type=jnp.float32)
    hidden = (jax.nn.silu(gate_act) * up_act).astype(jnp.bfloat16)
    return jnp.dot(hidden, down_rows, preferred_element_type=jnp.float32)


def reference(hidden_in, expert_ids, gate_weights, replica_pick, placement, capacity, w_gate, w_up, w_down):
    slot_of = choose_slots(expert_ids, replica_pick, placement).reshape(-1)
    rank_of = rank_in_source(slot_of, TOK_DEV * TOP, NODES)
    kept_mask = rank_of < capacity[slot_of]
    token_of = (jnp.arange(TOKENS * TOP, dtype=jnp.int32) // TOP).astype(jnp.int32)
    source_of = (token_of // TOK_DEV).astype(jnp.int32)
    slot_span = N_NODE * CAP
    cell_count = NODES * slot_span
    cell_of = (slot_of * slot_span + source_of * CAP + rank_of).astype(jnp.int32)
    target = jnp.where(kept_mask, cell_of, cell_count).astype(jnp.int32)
    table_tok = jnp.full((cell_count,), TOKENS, jnp.int32).at[target].set(token_of, mode="drop")
    table_weight = jnp.zeros((cell_count,), jnp.float32).at[target].set(gate_weights.reshape(-1), mode="drop")
    padded = jnp.concatenate([hidden_in, jnp.zeros((1, D), hidden_in.dtype)], axis=0)

    def one_slot(totals, slot_index):
        tokens_here = lax.dynamic_slice_in_dim(table_tok, slot_index * slot_span, slot_span)
        weights_here = lax.dynamic_slice_in_dim(table_weight, slot_index * slot_span, slot_span)
        row_block = padded[tokens_here]
        gate_cols = lax.dynamic_slice_in_dim(w_gate, slot_index * FW, FW, 1)
        up_cols = lax.dynamic_slice_in_dim(w_up, slot_index * FW, FW, 1)
        down_rows = lax.dynamic_slice_in_dim(w_down, slot_index * FW, FW, 0)
        expert_out = lax.optimization_barrier(expert_rows(row_block, gate_cols, up_cols, down_rows).astype(jnp.bfloat16))
        totals = totals.at[tokens_here].add(weights_here[:, None] * expert_out.astype(jnp.float32), mode="drop")
        return totals, None

    totals, unused = lax.scan(one_slot, jnp.zeros((TOKENS, D), jnp.float32), jnp.arange(NODES, dtype=jnp.int32))
    return totals.astype(jnp.bfloat16)
```

```python
import functools

import jax
import jax.numpy as jnp
from jax import lax
from jax.sharding import PartitionSpec as P


def route(expert_ids, gate_weights, replica_pick, placement, capacity, slot_label):
    slots = placement.shape[0]
    ids = jnp.arange(slots, dtype=jnp.int32)
    same = (placement[:, None] == placement[None, :]) & (ids[None, :] < ids[:, None])
    turn = jnp.sum(same.astype(jnp.int32), axis=1)
    pick = (slot_label[:, None] == ids[None, :]).astype(jnp.int32)
    place_q = jnp.sum(pick * placement[None, :], axis=1)
    turn_q = jnp.sum(pick * turn[None, :], axis=1)
    cap_q = jnp.sum(pick * capacity[None, :], axis=1)
    match = expert_ids[:, :, None] == place_q[None, None, :]
    hosts = jnp.sum(match.astype(jnp.int32), axis=2)
    wanted = replica_pick % hosts
    chosen = match & (turn_q[None, None, :] == wanted[:, :, None])
    used = jnp.sum(chosen.astype(jnp.int32), axis=1)
    weight = jnp.sum(jnp.where(chosen, gate_weights[:, :, None], 0.0), axis=1)
    toks = jnp.arange(expert_ids.shape[0], dtype=jnp.int32)
    rank = jnp.sum(jnp.where((toks[None, :] < toks[:, None])[:, :, None], used[None, :, :], 0), axis=1)
    kept = (used > 0) & (rank < cap_q[None, :])
    return kept, rank, weight


def per_device(
    hidden_in, expert_ids, gate_weights, replica_pick, placement, capacity, w_gate, w_up, w_down
):
    tok_rows, width = hidden_in.shape
    top = expert_ids.shape[1]
    slots = placement.shape[0]
    devices = lax.axis_size("node")
    members = devices // slots
    cells = members * max(1, tok_rows * top // (slots * members))
    bf16, f32 = jnp.bfloat16, jnp.float32
    my_slot = lax.axis_index("node") // members
    order = jnp.arange(slots, dtype=jnp.int32)

    def send(value, flip):
        return lax.ppermute(value, "node", [(d, d ^ flip) for d in range(devices)])

    kept, rank, weight = route(
        expert_ids, gate_weights, replica_pick, placement, capacity, order ^ my_slot
    )
    cell = jnp.arange(cells, dtype=jnp.int32)
    spot = kept.T[:, None, :] & (rank.T[:, None, :] == cell[None, :, None])
    pack = spot.astype(bf16).reshape(slots * cells, tok_rows)
    scale = jnp.where(spot, weight.T[:, None, :], 0.0).reshape(slots * cells, tok_rows).T
    packed = jnp.dot(pack, hidden_in, preferred_element_type=f32).astype(bf16)
    packed = packed.reshape(slots, cells, width)
    parts = [packed[q] if q == 0 else send(packed[q], q * members) for q in range(slots)]
    mine = jnp.concatenate(parts, axis=0)
    flips = [2, 1]
    rows = mine
    for flip in flips:
        rows = jnp.concatenate([rows, send(rows, flip)], axis=0)
    gate_act = jnp.dot(rows, w_gate, preferred_element_type=f32)
    up_act = jnp.dot(rows, w_up, preferred_element_type=f32)
    hid = (jax.nn.silu(gate_act) * up_act).astype(bf16)
    out = jnp.dot(hid, w_down, preferred_element_type=f32)
    for flip in reversed(flips):
        half = out.shape[0] // 2
        out = out[:half] + send(out[half:].astype(bf16), flip).astype(f32)
    out = out.astype(bf16).reshape(slots, cells, width)
    back = [out[q] if q == 0 else send(out[q], q * members) for q in range(slots)]
    back = jnp.concatenate(back, axis=0)
    mixed = jnp.dot(scale, back.astype(f32), precision=lax.Precision.HIGHEST, preferred_element_type=f32)
    return mixed.astype(bf16)


def solution(mesh):
    split = P(("grp", "node"), None)
    placed = (split, split, split, split, P(), P(), P(None, "node"), P(None, "node"), P("node", None))
    return jax.shard_map(per_device, mesh=mesh, in_specs=placed, out_specs=split, check_vma=False)
```

```python
import functools

import jax
import jax.numpy as jnp
from jax import lax
from jax.experimental import pallas as pl
from jax.experimental.pallas import tpu as pltpu
from jax.sharding import PartitionSpec as P

BF16, F32, I32 = jnp.bfloat16, jnp.float32, jnp.int32
VMEM = pl.BlockSpec(memory_space=pltpu.VMEM)
SMEM = pl.BlockSpec(memory_space=pltpu.SMEM)
HBM = pl.BlockSpec(memory_space=pltpu.HBM)


def shape(dims, dtype):
    return jax.ShapeDtypeStruct(dims, dtype)


def call(kernel, outs, ins, name, flops=0, moved=0, limit=24, scratch=()):
    return pl.pallas_call(
        kernel,
        out_shape=outs,
        in_specs=ins,
        out_specs=[VMEM] * len(outs),
        scratch_shapes=list(scratch),
        compiler_params=pltpu.CompilerParams(vmem_limit_bytes=limit << 20),
        cost_estimate=pl.CostEstimate(flops=flops, bytes_accessed=moved, transcendentals=0),
        name=name,
    )


def cuts(width, count):
    tiles = width // 128
    edges = [128 * (tiles * i // count) for i in range(count + 1)]
    return list(zip(edges[:-1], edges[1:]))


def route_kernel(cells, ranges, slot_ref, ids_ref, gate_ref, pick_ref, place_ref, cap_ref, rows_ref, *outs):
    top, toks = ids_ref.shape
    slots = place_ref.shape[1]
    total = slots * cells
    cell = lax.broadcasted_iota(I32, (total, slots), 0)
    slot = lax.broadcasted_iota(I32, (total, slots), 1)
    label = jnp.bitwise_xor(cell // cells, slot_ref[0])
    here = slot == label
    place = jnp.broadcast_to(place_ref[...], (total, slots))
    caps = jnp.broadcast_to(cap_ref[...], (total, slots))
    place_c = jnp.sum(jnp.where(here, place, 0), axis=1, keepdims=True)
    cap_c = jnp.sum(jnp.where(here, caps, 0), axis=1, keepdims=True)
    same = place == place_c
    turn_c = jnp.sum(jnp.where(same & (slot < label), 1, 0), axis=1, keepdims=True)
    hosts_c = jnp.sum(jnp.where(same, 1, 0), axis=1, keepdims=True).astype(F32)
    used = jnp.zeros((total, toks), F32)
    weight = jnp.zeros((total, toks), F32)
    for k in range(top):
        pick = pick_ref[k : k + 1, :].astype(F32)
        wanted = pick - hosts_c * jnp.floor((pick + 0.5) / hosts_c)
        chosen = (ids_ref[k : k + 1, :] == place_c) & (wanted.astype(I32) == turn_c)
        used = jnp.where(chosen, 1.0, used)
        weight = jnp.where(chosen, gate_ref[k : k + 1, :], weight)
    earlier = lax.broadcasted_iota(I32, (toks, toks), 0) < lax.broadcasted_iota(I32, (toks, toks), 1)
    rank = jnp.dot(used, earlier.astype(F32), preferred_element_type=F32).astype(I32)
    seat = lax.broadcasted_iota(I32, (total, toks), 0) % cells
    spot = (used > 0.5) & (rank < cap_c) & (rank == seat)
    outs[-1][...] = jnp.where(spot, weight, 0.0)
    pack = spot.astype(F32).astype(BF16)
    high = slots // 2
    block = 2 * cells
    for i, (lo, hi) in enumerate(ranges):
        packed = jnp.dot(pack, rows_ref[:, lo:hi], preferred_element_type=F32)
        for z in range(high):
            outs[i * high + z][...] = packed[z * block : (z + 1) * block].astype(BF16)


def split_kernel(cells, *refs):
    ins, (own_ref, oth_ref) = refs[:-2], refs[-2:]
    vals = [r[...].astype(F32) for r in ins]
    own_ref[...] = jnp.concatenate([v[:cells] for v in vals], axis=0).astype(BF16)
    oth_ref[...] = jnp.concatenate([v[cells:] for v in vals], axis=0).astype(BF16)


def merge_kernel(cells, keep_ref, core_ref, x_ref, y_ref, d_ref, *outs):
    own = keep_ref[...] + core_ref[...].astype(F32) + x_ref[...].astype(F32)
    oth = y_ref[...].astype(F32) + d_ref[...].astype(F32)
    for z, out in enumerate(outs):
        part = slice(z * cells, (z + 1) * cells)
        out[...] = jnp.concatenate([own[part], oth[part]], axis=0).astype(BF16)


def fetch_kernel(count, *refs):
    ins, outs, sem = refs[:count], refs[count : 2 * count], refs[2 * count]
    copies = [pltpu.make_async_copy(a, b, sem.at[i]) for i, (a, b) in enumerate(zip(ins, outs))]
    for c in copies:
        c.start()
    for c in copies:
        c.wait()


def up_kernel(blocks, base, first, last, *refs):
    rows, rest = refs[:blocks], refs[blocks:]
    gate_ref, up_ref, rest = rest[0], rest[1], rest[2:]
    if first:
        old_g = old_u = None
    else:
        old_g, old_u, rest = rest[0], rest[1], rest[2:]
    if last:
        hid_ref, acc_g, acc_u = rest
    else:
        acc_g, acc_u = rest
    width = rows[0].shape[1]
    if first:
        acc_g[...] = jnp.zeros_like(acc_g)
        acc_u[...] = jnp.zeros_like(acc_u)
    else:
        acc_g[...] = old_g[...]
        acc_u[...] = old_u[...]
    step = 512 if width % 512 == 0 else (256 if width % 256 == 0 else 128)

    def body(i, unused):
        at = pl.multiple_of(i * step, step)
        x = jnp.concatenate([r[:, pl.ds(at, step)] for r in rows], axis=0)
        wat = pl.multiple_of(base + i * step, 128)
        acc_g[...] += jnp.dot(x, gate_ref[pl.ds(wat, step), :], preferred_element_type=F32)
        acc_u[...] += jnp.dot(x, up_ref[pl.ds(wat, step), :], preferred_element_type=F32)
        return unused

    lax.fori_loop(0, width // step, body, 0)
    if last:
        g = acc_g[...]
        hid_ref[...] = (g / (1.0 + jnp.exp(-g)) * acc_u[...]).astype(BF16)


def down_kernel(base, width, hid_ref, down_ref, *outs):
    step = 512 if width % 512 == 0 else (256 if width % 256 == 0 else 128)
    rows = outs[0].shape[0]

    def body(i, unused):
        at = pl.multiple_of(i * step, step)
        wat = pl.multiple_of(base + i * step, 128)
        val = jnp.dot(hid_ref[...], down_ref[:, pl.ds(wat, step)], preferred_element_type=F32)
        for b, out in enumerate(outs):
            out[:, pl.ds(at, step)] = val[b * rows : (b + 1) * rows].astype(out.dtype)
        return unused

    lax.fori_loop(0, width // step, body, 0)


def combine_kernel(high, ranges, scale_ref, *refs):
    out_ref = refs[-1]
    toks = scale_ref.shape[0]
    s = scale_ref[...]
    a = s.astype(BF16)
    left = s - a.astype(F32)
    b = left.astype(BF16)
    c = (left - b.astype(F32)).astype(BF16)
    pieces = jnp.concatenate([v.astype(F32) for v in (a, b, c)], axis=0).astype(BF16)
    for i, (lo, hi) in enumerate(ranges):
        rows = jnp.concatenate([r[...].astype(F32) for r in refs[i * high : (i + 1) * high]], axis=0)
        val = jnp.dot(pieces, rows.astype(BF16), preferred_element_type=F32)
        val = val[:toks] + val[toks : 2 * toks] + val[2 * toks :]
        out_ref[:, lo:hi] = val.astype(BF16)


def per_device(n_in, n_out, hidden_in, expert_ids, gate_weights, replica_pick, placement, capacity, w_gate, w_up, w_down):
    toks, width = hidden_in.shape
    top = expert_ids.shape[1]
    slots = placement.shape[0]
    devices = lax.axis_size("node")
    members = devices // slots
    cells = members * max(1, toks * top // (slots * members))
    high = slots // 2
    fw = w_gate.shape[1]
    rows = high * cells
    my_slot = lax.axis_index("node") // members

    def send(value, flip):
        return lax.ppermute(value, "node", [(d, d ^ flip) for d in range(devices)])

    in_cuts, out_cuts = cuts(width, n_in), cuts(width, n_out)
    route = call(
        functools.partial(route_kernel, cells, in_cuts),
        [shape((2 * cells, hi - lo), BF16) for lo, hi in in_cuts for z in range(high)]
        + [shape((slots * cells, toks), F32)],
        [SMEM] + [VMEM] * 6,
        "route",
    )(my_slot.reshape(1).astype(I32), expert_ids.T, gate_weights.T, replica_pick.T, placement[None, :], capacity[None, :], hidden_in)
    scale = route[-1].T
    wg, wu, wd = call(
        functools.partial(fetch_kernel, 3),
        [shape(w.shape, BF16) for w in (w_gate, w_up, w_down)],
        [HBM] * 3,
        "fetch",
        moved=6 * w_gate.size * 2,
        limit=1,
        scratch=[pltpu.SemaphoreType.DMA((3,))],
    )(w_gate, w_up, w_down)
    acc = ()
    z_order = list(range(high - 1, 0, -1))
    for i, (lo, hi) in enumerate(in_cuts):
        base = route[i * high : (i + 1) * high]
        blocks = {z: send(base[z], 2 * members * z) for z in z_order}
        blocks[0] = base[0]
        own, oth = call(
            functools.partial(split_kernel, cells),
            [shape((rows, hi - lo), BF16)] * 2,
            [VMEM] * high,
            "split",
        )(*[blocks[z] for z in range(high)])
        group = [own, send(own, 2), send(oth, members), send(oth, members + 2)]
        group = group + [send(g, 1) for g in group]
        first, last = i == 0, i == n_in - 1
        acc = call(
            functools.partial(up_kernel, 8, lo, first, last),
            ([shape((8 * rows, fw), BF16)] if last else []) + [shape((8 * rows, fw), F32)] * 2,
            [VMEM] * (10 + len(acc)),
            "up",
            flops=4 * 8 * rows * fw * (hi - lo),
        )(*group, wg, wu, *acc)
    hid = acc[0]
    finals = []
    for lo, hi in out_cuts:
        outs = call(
            functools.partial(down_kernel, lo, hi - lo),
            [shape((rows, hi - lo), F32)] * 4 + [shape((rows, hi - lo), BF16)] * 4,
            [VMEM] * 2,
            "down",
            flops=2 * 8 * rows * fw * (hi - lo),
        )(hid, wd)
        keep, give = outs[:4], outs[4:]
        got = [send(give[b], 1) for b in (3, 2, 1, 0)][::-1]
        half = [(keep[b] + got[b].astype(F32)).astype(BF16) for b in (1, 2, 3)]
        dg, yg, xg = send(half[2], members + 2), send(half[1], members), send(half[0], 2)
        done = call(
            functools.partial(merge_kernel, cells),
            [shape((2 * cells, hi - lo), BF16)] * high,
            [VMEM] * 5,
            "merge",
        )(keep[0], got[0], xg, yg, dg)
        back = {z: send(done[z], 2 * members * z) for z in z_order}
        back[0] = done[0]
        finals += [back[z] for z in range(high)]
    (mixed,) = call(
        functools.partial(combine_kernel, high, out_cuts),
        [shape((toks, width), BF16)],
        [VMEM] * (1 + len(finals)),
        "combine",
    )(scale, *finals)
    return mixed


def solution(mesh):
    split = P(("grp", "node"), None)
    placed = (split, split, split, split, P(), P(), P(None, "node"), P(None, "node"), P("node", None))
    body = functools.partial(per_device, 1, 1)
    return jax.shard_map(body, mesh=mesh, in_specs=placed, out_specs=split, check_vma=False)
```

```python
import functools

import jax
import jax.numpy as jnp
from jax import lax
from jax.experimental import pallas as pl
from jax.experimental.pallas import tpu as pltpu
from jax.sharding import PartitionSpec as P

BF16, F32, I32 = jnp.bfloat16, jnp.float32, jnp.int32
VMEM = pl.BlockSpec(memory_space=pltpu.VMEM)
SMEM = pl.BlockSpec(memory_space=pltpu.SMEM)
HBM = pl.BlockSpec(memory_space=pltpu.HBM)


def shape(dims, dtype):
    return jax.ShapeDtypeStruct(dims, dtype)


def call(kernel, outs, ins, name, flops=0, moved=0, limit=24, scratch=()):
    return pl.pallas_call(
        kernel,
        out_shape=outs,
        in_specs=ins,
        out_specs=[VMEM] * len(outs),
        scratch_shapes=list(scratch),
        compiler_params=pltpu.CompilerParams(vmem_limit_bytes=limit << 20),
        cost_estimate=pl.CostEstimate(flops=flops, bytes_accessed=moved, transcendentals=0),
        name=name,
    )


def cuts(width, count):
    tiles = width // 128
    edges = [128 * (tiles * i // count) for i in range(count + 1)]
    return list(zip(edges[:-1], edges[1:]))


def sweep(part, base, width, unrolled):
    step = max(t for t in (1024, 896, 512, 256, 128) if width % t == 0)
    if unrolled:
        for at in range(0, width, step):
            part(at, base + at, step)
        return

    def body(i, unused):
        part(pl.multiple_of(i * step, 128), pl.multiple_of(base + i * step, 128), step)
        return unused

    lax.fori_loop(0, width // step, body, 0)


def route_kernel(cells, ranges, slot_ref, *refs):
    ins, outs, held, sem = refs[:6], refs[6:-7], refs[-7:-1], refs[-1]
    copies = [pltpu.make_async_copy(a, b, sem.at[i]) for i, (a, b) in enumerate(zip(ins, held))]
    for c in copies:
        c.start()
    for c in copies:
        c.wait()
    ids_ref, gate_ref, pick_ref, place_ref, cap_ref, rows_ref = held
    top, toks = ids_ref.shape
    slots = place_ref.shape[1]
    total = slots * cells
    cell = lax.broadcasted_iota(I32, (total, slots), 0)
    slot = lax.broadcasted_iota(I32, (total, slots), 1)
    label = jnp.bitwise_xor(cell // cells, slot_ref[0])
    here = slot == label
    place = jnp.broadcast_to(place_ref[...], (total, slots))
    caps = jnp.broadcast_to(cap_ref[...], (total, slots))
    place_c = jnp.sum(jnp.where(here, place, 0), axis=1, keepdims=True)
    cap_c = jnp.sum(jnp.where(here, caps, 0), axis=1, keepdims=True)
    same = place == place_c
    turn_c = jnp.sum(jnp.where(same & (slot < label), 1, 0), axis=1, keepdims=True)
    hosts_c = jnp.sum(jnp.where(same, 1, 0), axis=1, keepdims=True).astype(F32)
    used = jnp.zeros((total, toks), F32)
    weight = jnp.zeros((total, toks), F32)
    for k in range(top):
        pick = pick_ref[k : k + 1, :].astype(F32)
        wanted = pick - hosts_c * jnp.floor((pick + 0.5) / hosts_c)
        chosen = (ids_ref[k : k + 1, :] == place_c) & (wanted.astype(I32) == turn_c)
        used = jnp.where(chosen, 1.0, used)
        weight = jnp.where(chosen, gate_ref[k : k + 1, :], weight)
    earlier = lax.broadcasted_iota(I32, (toks, toks), 0) < lax.broadcasted_iota(I32, (toks, toks), 1)
    rank = jnp.dot(used, earlier.astype(F32), preferred_element_type=F32).astype(I32)
    seat = lax.broadcasted_iota(I32, (total, toks), 0) % cells
    spot = (used > 0.5) & (rank < cap_c) & (rank == seat)
    outs[-1][...] = jnp.where(spot, weight, 0.0)
    pack = spot.astype(F32).astype(BF16)
    high = slots // 2
    block = 2 * cells
    for i, (lo, hi) in enumerate(ranges):
        packed = jnp.dot(pack, rows_ref[:, lo:hi], preferred_element_type=F32)
        for z in range(high):
            outs[i * high + z][...] = packed[z * block : (z + 1) * block].astype(BF16)


def split_kernel(cells, *refs):
    ins, (own_ref, oth_ref) = refs[:-3], refs[-2:]
    vals = [r[...].astype(F32) for r in ins]
    own_ref[...] = jnp.concatenate([v[:cells] for v in vals], axis=0).astype(BF16)
    oth_ref[...] = jnp.concatenate([v[cells:] for v in vals], axis=0).astype(BF16)


def merge_kernel(cells, keep_ref, core_ref, x_ref, y_ref, d_ref, *outs):
    own = keep_ref[...] + core_ref[...].astype(F32) + x_ref[...].astype(F32)
    oth = y_ref[...].astype(F32) + d_ref[...].astype(F32)
    for z, out in enumerate(outs):
        part = slice(z * cells, (z + 1) * cells)
        out[...] = jnp.concatenate([own[part], oth[part]], axis=0).astype(BF16)


def fetch_kernel(count, *refs):
    ins, outs, sem = refs[:count], refs[count + 1 : 2 * count + 1], refs[2 * count + 1]
    copies = [pltpu.make_async_copy(a, b, sem.at[i]) for i, (a, b) in enumerate(zip(ins, outs))]
    for c in copies:
        c.start()
    for c in copies:
        c.wait()


def up_kernel(blocks, base, first, last, *refs):
    rows, rest = refs[:blocks], refs[blocks:]
    gate_ref, up_ref, rest = rest[0], rest[1], rest[2:]
    if first:
        old_g = old_u = None
    else:
        old_g, old_u, rest = rest[0], rest[1], rest[2:]
    if last:
        hid_ref, acc_g, acc_u = rest
    else:
        acc_g, acc_u = rest
    width = rows[0].shape[1]
    if first:
        acc_g[...] = jnp.zeros_like(acc_g)
        acc_u[...] = jnp.zeros_like(acc_u)
    else:
        acc_g[...] = old_g[...]
        acc_u[...] = old_u[...]

    def part(at, wat, step):
        x = jnp.concatenate([r[:, pl.ds(at, step)] for r in rows], axis=0)
        acc_g[...] += jnp.dot(x, gate_ref[pl.ds(wat, step), :], preferred_element_type=F32)
        acc_u[...] += jnp.dot(x, up_ref[pl.ds(wat, step), :], preferred_element_type=F32)

    sweep(part, base, width, blocks * rows[0].shape[0] <= 256)
    if last:
        g = acc_g[...]
        hid_ref[...] = (g / (1.0 + jnp.exp(-g)) * acc_u[...]).astype(BF16)


def down_kernel(base, width, hid_ref, down_ref, *outs):
    rows = outs[0].shape[0]

    def part(at, wat, step):
        val = jnp.dot(hid_ref[...], down_ref[:, pl.ds(wat, step)], preferred_element_type=F32)
        for b, out in enumerate(outs):
            out[:, pl.ds(at, step)] = val[b * rows : (b + 1) * rows].astype(out.dtype)

    sweep(part, base, width, len(outs) * rows <= 256)


def combine_kernel(high, ranges, scale_ref, *refs):
    out_ref = refs[-1]
    toks = scale_ref.shape[0]
    s = scale_ref[...]
    a = s.astype(BF16)
    left = s - a.astype(F32)
    b = left.astype(BF16)
    c = (left - b.astype(F32)).astype(BF16)
    pieces = jnp.concatenate([v.astype(F32) for v in (a, b, c)], axis=0).astype(BF16)
    for i, (lo, hi) in enumerate(ranges):
        rows = jnp.concatenate([r[...].astype(F32) for r in refs[i * high : (i + 1) * high]], axis=0)
        val = jnp.dot(pieces, rows.astype(BF16), preferred_element_type=F32)
        val = val[:toks] + val[toks : 2 * toks] + val[2 * toks :]
        out_ref[:, lo:hi] = val.astype(BF16)


def per_device(n_in, n_out, hidden_in, expert_ids, gate_weights, replica_pick, placement, capacity, w_gate, w_up, w_down):
    toks, width = hidden_in.shape
    top = expert_ids.shape[1]
    slots = placement.shape[0]
    devices = lax.axis_size("node")
    members = devices // slots
    cells = members * max(1, toks * top // (slots * members))
    high = slots // 2
    fw = w_gate.shape[1]
    rows = high * cells
    my_slot = lax.axis_index("node") // members

    def send(value, flip):
        return lax.ppermute(value, "node", [(d, d ^ flip) for d in range(devices)])

    in_cuts, out_cuts = cuts(width, n_in), cuts(width, n_out)
    inputs = (expert_ids.T, gate_weights.T, replica_pick.T, placement[None, :], capacity[None, :], hidden_in)
    route = call(
        functools.partial(route_kernel, cells, in_cuts),
        [shape((2 * cells, hi - lo), BF16) for lo, hi in in_cuts for z in range(high)]
        + [shape((slots * cells, toks), F32)],
        [SMEM] + [HBM] * 6,
        "route",
        limit=60,
        scratch=[pltpu.VMEM(a.shape, a.dtype) for a in inputs] + [pltpu.SemaphoreType.DMA((6,))],
    )(my_slot.reshape(1).astype(I32), *inputs)
    scale = route[-1].T
    wg, wu, wd = call(
        functools.partial(fetch_kernel, 3),
        [shape(w.shape, BF16) for w in (w_gate, w_up, w_down)],
        [HBM] * 4,
        "fetch",
        moved=6 * w_gate.size * 2,
        limit=40,
        scratch=[pltpu.SemaphoreType.DMA((3,))],
    )(w_gate, w_up, w_down, route[-1])
    acc = ()
    z_order = list(range(high - 1, 0, -1))
    for i, (lo, hi) in enumerate(in_cuts):
        base = route[i * high : (i + 1) * high]
        blocks = {z: send(base[z], 2 * members * z) for z in z_order}
        blocks[0] = base[0]
        own, oth = call(
            functools.partial(split_kernel, cells),
            [shape((rows, hi - lo), BF16)] * 2,
            [VMEM] * high + [pl.BlockSpec(memory_space=pl.ANY)],
            "split",
        )(*[blocks[z] for z in range(high)], wd)
        group = [own, send(own, 2), send(oth, members), send(oth, members + 2)]
        group = group + [send(g, 1) for g in group]
        first, last = i == 0, i == n_in - 1
        acc = call(
            functools.partial(up_kernel, 8, lo, first, last),
            ([shape((8 * rows, fw), BF16)] if last else []) + [shape((8 * rows, fw), F32)] * 2,
            [VMEM] * (10 + len(acc)),
            "up",
            flops=4 * 8 * rows * fw * (hi - lo),
        )(*group, wg, wu, *acc)
    hid = acc[0]
    finals = []
    for lo, hi in out_cuts:
        outs = call(
            functools.partial(down_kernel, lo, hi - lo),
            [shape((rows, hi - lo), F32)] * 4 + [shape((rows, hi - lo), BF16)] * 4,
            [VMEM] * 2,
            "down",
            flops=2 * 8 * rows * fw * (hi - lo),
        )(hid, wd)
        keep, give = outs[:4], outs[4:]
        got = [send(give[b], 1) for b in (3, 2, 1, 0)][::-1]
        half = [(keep[b] + got[b].astype(F32)).astype(BF16) for b in (1, 2, 3)]
        dg, yg, xg = send(half[2], members + 2), send(half[1], members), send(half[0], 2)
        done = call(
            functools.partial(merge_kernel, cells),
            [shape((2 * cells, hi - lo), BF16)] * high,
            [VMEM] * 5,
            "merge",
        )(keep[0], got[0], xg, yg, dg)
        back = {z: send(done[z], 2 * members * z) for z in z_order}
        back[0] = done[0]
        finals += [back[z] for z in range(high)]
    (mixed,) = call(
        functools.partial(combine_kernel, high, out_cuts),
        [shape((toks, width), BF16)],
        [VMEM] * (1 + len(finals)),
        "combine",
    )(scale, *finals)
    return mixed


def solution(mesh):
    split = P(("grp", "node"), None)
    placed = (split, split, split, split, P(), P(), P(None, "node"), P(None, "node"), P("node", None))
    body = functools.partial(per_device, 1, 2)
    return jax.shard_map(body, mesh=mesh, in_specs=placed, out_specs=split, check_vma=False)
```

```python
import functools

import jax
import jax.numpy as jnp
from jax import lax
from jax.experimental import pallas as pl
from jax.experimental.pallas import tpu as pltpu
from jax.sharding import PartitionSpec as P

BF16, F32, I32 = jnp.bfloat16, jnp.float32, jnp.int32
VMEM = pl.BlockSpec(memory_space=pltpu.VMEM)
SMEM = pl.BlockSpec(memory_space=pltpu.SMEM)
HBM = pl.BlockSpec(memory_space=pltpu.HBM)


def shape(dims, dtype):
    return jax.ShapeDtypeStruct(dims, dtype)


def call(kernel, outs, ins, name, flops=0, moved=0, limit=24, scratch=()):
    return pl.pallas_call(
        kernel,
        out_shape=outs,
        in_specs=ins,
        out_specs=[VMEM] * len(outs),
        scratch_shapes=list(scratch),
        compiler_params=pltpu.CompilerParams(vmem_limit_bytes=limit << 20),
        cost_estimate=pl.CostEstimate(flops=flops, bytes_accessed=moved, transcendentals=0),
        name=name,
    )


def sweep(part, base, width, unrolled):
    step = max(t for t in (1024, 896, 512, 256, 128) if width % t == 0)
    if unrolled:
        for at in range(0, width, step):
            part(at, base + at, step)
        return

    def body(i, unused):
        part(pl.multiple_of(i * step, 128), pl.multiple_of(base + i * step, 128), step)
        return unused

    lax.fori_loop(0, width // step, body, 0)


def route_kernel(cells, ranges, slot_ref, *refs):
    ins, outs, held, sem = refs[:6], refs[6:-7], refs[-7:-1], refs[-1]
    copies = [pltpu.make_async_copy(a, b, sem.at[i]) for i, (a, b) in enumerate(zip(ins, held))]
    for c in copies:
        c.start()
    for c in copies:
        c.wait()
    ids_ref, gate_ref, pick_ref, place_ref, cap_ref, rows_ref = held
    top, toks = ids_ref.shape
    slots = place_ref.shape[1]
    total = slots * cells
    cell = lax.broadcasted_iota(I32, (total, slots), 0)
    slot = lax.broadcasted_iota(I32, (total, slots), 1)
    label = jnp.bitwise_xor(cell // cells, slot_ref[0])
    here = slot == label
    place = jnp.broadcast_to(place_ref[...], (total, slots))
    caps = jnp.broadcast_to(cap_ref[...], (total, slots))
    place_c = jnp.sum(jnp.where(here, place, 0), axis=1, keepdims=True)
    cap_c = jnp.sum(jnp.where(here, caps, 0), axis=1, keepdims=True)
    same = place == place_c
    turn_c = jnp.sum(jnp.where(same & (slot < label), 1, 0), axis=1, keepdims=True)
    hosts_c = jnp.sum(jnp.where(same, 1, 0), axis=1, keepdims=True).astype(F32)
    used = jnp.zeros((total, toks), F32)
    weight = jnp.zeros((total, toks), F32)
    for k in range(top):
        pick = pick_ref[k : k + 1, :].astype(F32)
        wanted = pick - hosts_c * jnp.floor((pick + 0.5) / hosts_c)
        chosen = (ids_ref[k : k + 1, :] == place_c) & (wanted.astype(I32) == turn_c)
        used = jnp.where(chosen, 1.0, used)
        weight = jnp.where(chosen, gate_ref[k : k + 1, :], weight)
    earlier = lax.broadcasted_iota(I32, (toks, toks), 0) < lax.broadcasted_iota(I32, (toks, toks), 1)
    rank = jnp.dot(used, earlier.astype(F32), preferred_element_type=F32).astype(I32)
    seat = lax.broadcasted_iota(I32, (total, toks), 0) % cells
    spot = (used > 0.5) & (rank < cap_c) & (rank == seat)
    outs[-1][...] = jnp.where(spot, weight, 0.0)
    pack = spot.astype(F32).astype(BF16)
    high = slots // 2
    block = 2 * cells
    for i, (lo, hi) in enumerate(ranges):
        packed = jnp.dot(pack, rows_ref[:, lo:hi], preferred_element_type=F32)
        for z in range(high):
            outs[i * high + z][...] = packed[z * block : (z + 1) * block].astype(BF16)


def split_kernel(cells, count, *refs):
    own_ref, oth_ref = refs[-2:]
    vals = [r[...].astype(F32) for r in refs[:count]]
    own_ref[...] = jnp.concatenate([v[:cells] for v in vals], axis=0).astype(BF16)
    oth_ref[...] = jnp.concatenate([v[cells:] for v in vals], axis=0).astype(BF16)


def join_kernel(count, *refs):
    refs[-1][...] = jnp.concatenate([r[...].astype(F32) for r in refs[:count]], axis=0).astype(BF16)


def half_kernel(keep_ref, core_ref, *refs):
    outs = refs[-4:]
    rows = outs[0].shape[0]
    for i, out in enumerate(outs):
        part = slice(i * rows, (i + 1) * rows)
        out[...] = (keep_ref[part, :] + core_ref[...].astype(F32)[part]).astype(out.dtype)


def merge_kernel(cells, own_ref, x_ref, y_ref, d_ref, *outs):
    own = own_ref[...] + x_ref[...].astype(F32)
    oth = y_ref[...].astype(F32) + d_ref[...].astype(F32)
    for z, out in enumerate(outs):
        part = slice(z * cells, (z + 1) * cells)
        out[...] = jnp.concatenate([own[part], oth[part]], axis=0).astype(BF16)


def fetch_kernel(count, *refs):
    ins, outs, sem = refs[:count], refs[count + 1 : 2 * count + 1], refs[2 * count + 1]
    copies = [pltpu.make_async_copy(a, b, sem.at[i]) for i, (a, b) in enumerate(zip(ins, outs))]
    for c in copies:
        c.start()
    for c in copies:
        c.wait()


def up_kernel(near, far, *refs):
    rows, (gate_ref, up_ref), (far_hid, near_hid, acc_g, acc_u) = refs[:4], refs[4:6], refs[6:]
    acc_g[...] = jnp.zeros_like(acc_g)
    acc_u[...] = jnp.zeros_like(acc_u)

    def part(at, wat, step):
        x = jnp.concatenate([r[:, pl.ds(at, step)] for r in rows], axis=0)
        acc_g[...] += jnp.dot(x, gate_ref[pl.ds(wat, step), :], preferred_element_type=F32)
        acc_u[...] += jnp.dot(x, up_ref[pl.ds(wat, step), :], preferred_element_type=F32)

    sweep(part, 0, rows[0].shape[1], acc_g.shape[0] <= 256)
    g = acc_g[...]
    hid = (g / (1.0 + jnp.exp(-g)) * acc_u[...]).astype(BF16)
    far_hid[...] = hid[:far]
    near_hid[...] = hid[far:]


def down_kernel(hid_ref, down_ref, keep_ref, give_ref):
    rows = keep_ref.shape[0]

    def part(at, wat, step):
        val = jnp.dot(hid_ref[...], down_ref[:, pl.ds(wat, step)], preferred_element_type=F32)
        keep_ref[:, pl.ds(at, step)] = val[:rows]
        give_ref[:, pl.ds(at, step)] = val[rows:].astype(BF16)

    sweep(part, 0, keep_ref.shape[1], rows <= 128)


def combine_kernel(scale_ref, *refs):
    out_ref = refs[-1]
    toks = scale_ref.shape[0]
    s = scale_ref[...]
    a = s.astype(BF16)
    left = s - a.astype(F32)
    b = left.astype(BF16)
    c = (left - b.astype(F32)).astype(BF16)
    pieces = jnp.concatenate([v.astype(F32) for v in (a, b, c)], axis=0).astype(BF16)
    rows = jnp.concatenate([r[...].astype(F32) for r in refs[:-1]], axis=0).astype(BF16)
    val = jnp.dot(pieces, rows, preferred_element_type=F32)
    out_ref[...] = (val[:toks] + val[toks : 2 * toks] + val[2 * toks :]).astype(BF16)


def per_device(
    hidden_in, expert_ids, gate_weights, replica_pick, placement, capacity, w_gate, w_up, w_down
):
    toks, width = hidden_in.shape
    top = expert_ids.shape[1]
    slots = placement.shape[0]
    devices = lax.axis_size("node")
    members = devices // slots
    cells = members * max(1, toks * top // (slots * members))
    high = slots // 2
    fw = w_gate.shape[1]
    my_slot = lax.axis_index("node") // members
    near, far = range(high // 2), range(high // 2, high)
    rows = high // 2 * cells
    any_ref = pl.BlockSpec(memory_space=pl.ANY)

    def send(value, flip):
        return lax.ppermute(value, "node", [(d, d ^ flip) for d in range(devices)])

    def over_z(block, z):
        return block if z == 0 else send(block, 2 * members * z)

    def split(blocks, when):
        return call(
            functools.partial(split_kernel, cells, len(blocks)),
            [shape((rows, width), BF16)] * 2,
            [VMEM] * len(blocks) + [any_ref] * len(when),
            "split",
        )(*blocks, *when)

    def spread(own, oth):
        d, y, x = send(oth, members + 2), send(oth, members), send(own, 2)
        return own, x, y, d

    def join(blocks, when):
        return call(
            functools.partial(join_kernel, 4),
            [shape((4 * rows, width), BF16)],
            [VMEM] * 4 + [any_ref] * len(when),
            "join",
        )(*blocks, *when)[0]

    inputs = (expert_ids.T, gate_weights.T, replica_pick.T, placement[None, :], capacity[None, :], hidden_in)
    route = call(
        functools.partial(route_kernel, cells, [(0, width)]),
        [shape((2 * cells, width), BF16)] * high + [shape((slots * cells, toks), F32)],
        [SMEM] + [HBM] * 6,
        "route",
        limit=60,
        scratch=[pltpu.VMEM(a.shape, a.dtype) for a in inputs] + [pltpu.SemaphoreType.DMA((6,))],
    )(my_slot.reshape(1).astype(I32), *inputs)
    scale = route[-1].T
    near_z = [over_z(route[z], z) for z in near]
    far_z = [over_z(route[z], z) for z in far]
    near_own, near_oth = split(near_z, ())
    near_rows = spread(near_own, near_oth)
    far_own, far_oth = split(far_z, ())
    far_rows = spread(far_own, far_oth)
    near_all = join(near_rows, (far_own,))
    near_core = send(near_all, 1)
    wg, wu, wd = call(
        functools.partial(fetch_kernel, 3),
        [shape(w.shape, BF16) for w in (w_gate, w_up, w_down)],
        [HBM] * 4,
        "fetch",
        moved=6 * w_gate.size * 2,
        limit=40,
        scratch=[pltpu.SemaphoreType.DMA((3,))],
    )(w_gate, w_up, w_down, near_all)
    far_all = join(far_rows, (wd,))
    far_core = send(far_all, 1)
    far_hid, near_hid, _, _ = call(
        functools.partial(up_kernel, 8 * rows, 8 * rows),
        [shape((8 * rows, fw), BF16)] * 2 + [shape((16 * rows, fw), F32)] * 2,
        [VMEM] * 6,
        "up",
        flops=64 * rows * fw * width,
    )(far_all, far_core, near_all, near_core, wg, wu)

    def down(hid, when):
        return call(
            down_kernel,
            [shape((4 * rows, width), F32), shape((4 * rows, width), BF16)],
            [VMEM] * 2 + [any_ref] * len(when),
            "down",
            flops=16 * rows * fw * width,
        )(hid, wd, *when)

    def half(keep, got, when):
        return call(
            half_kernel,
            [shape((rows, width), F32)] + [shape((rows, width), BF16)] * 3,
            [VMEM] * 2 + [any_ref] * len(when),
            "half",
        )(keep, got, *when)

    def merge(own, x, y, d):
        dg, yg, xg = send(d, members + 2), send(y, members), send(x, 2)
        return call(
            functools.partial(merge_kernel, cells),
            [shape((2 * cells, width), BF16)] * (high // 2),
            [VMEM] * 4,
            "merge",
        )(own, xg, yg, dg)

    far_keep, far_give = down(far_hid, ())
    far_got = send(far_give, 1)
    near_keep, near_give = down(near_hid, ())
    near_got = send(near_give, 1)
    far_done = merge(*half(far_keep, far_got, ()))
    far_back = [over_z(v, z) for v, z in zip(far_done, far)]
    near_done = merge(*half(near_keep, near_got, (far_done[0],)))
    near_back = [over_z(v, z) for v, z in zip(near_done, near)]
    (mixed,) = call(
        combine_kernel,
        [shape((toks, width), BF16)],
        [VMEM] * (1 + high),
        "combine",
    )(scale, *near_back, *far_back)
    return mixed


def solution(mesh):
    split = P(("grp", "node"), None)
    placed = (split, split, split, split, P(), P(), P(None, "node"), P(None, "node"), P("node", None))
    return jax.shard_map(per_device, mesh=mesh, in_specs=placed, out_specs=split, check_vma=False)
```

```python
import functools

import jax
import jax.numpy as jnp
from jax import lax
from jax.experimental import pallas as pl
from jax.experimental.pallas import tpu as pltpu
from jax.sharding import PartitionSpec as P

BF16, F32, I32 = jnp.bfloat16, jnp.float32, jnp.int32
VMEM = pl.BlockSpec(memory_space=pltpu.VMEM)
SMEM = pl.BlockSpec(memory_space=pltpu.SMEM)
HBM = pl.BlockSpec(memory_space=pltpu.HBM)


def shape(dims, dtype):
    return jax.ShapeDtypeStruct(dims, dtype)


def call(kernel, outs, ins, name, flops=0, moved=0, limit=24, scratch=()):
    return pl.pallas_call(
        kernel,
        out_shape=outs,
        in_specs=ins,
        out_specs=[VMEM] * len(outs),
        scratch_shapes=list(scratch),
        compiler_params=pltpu.CompilerParams(vmem_limit_bytes=limit << 20),
        cost_estimate=pl.CostEstimate(flops=flops, bytes_accessed=moved, transcendentals=0),
        name=name,
    )


def pieces(weights):
    a = weights.astype(BF16)
    b = (weights - a.astype(F32)).astype(BF16)
    c = (weights - a.astype(F32) - b.astype(F32)).astype(BF16)
    return a, b, c


def across(left, right):
    return lax.dot_general(left, right, (((0,), (0,)), ((), ())), preferred_element_type=F32)


def lane_slice(tail, start, count):
    lanes = tail.shape[1]
    place = lax.broadcasted_iota(I32, (lanes, count), 0) == lax.broadcasted_iota(I32, (lanes, count), 1) + start
    return jnp.dot(tail, jnp.where(place, 1.0, 0.0).astype(BF16), preferred_element_type=F32)


def sweep(part, base, width, unrolled):
    step = max(t for t in (1024, 896, 512, 256, 128) if width % t == 0)
    if unrolled:
        for at in range(0, width, step):
            part(at, base + at, step)
        return

    def body(i, unused):
        part(pl.multiple_of(i * step, 128), pl.multiple_of(base + i * step, 128), step)
        return unused

    lax.fori_loop(0, width // step, body, 0)


def route_kernel(cells, count, slot_ref, *refs):
    ins, outs, held, sem = refs[:6], refs[6:-7], refs[-7:-1], refs[-1]
    copies = [pltpu.make_async_copy(a, b, sem.at[i]) for i, (a, b) in enumerate(zip(ins, held))]
    for c in copies:
        c.start()
    for c in copies:
        c.wait()
    ids_ref, gate_ref, pick_ref, place_ref, cap_ref, rows_ref = held
    top, toks = ids_ref.shape
    slots = place_ref.shape[1]
    total = slots * cells
    cell = lax.broadcasted_iota(I32, (total, slots), 0)
    slot = lax.broadcasted_iota(I32, (total, slots), 1)
    label = jnp.bitwise_xor(cell // cells, slot_ref[0])
    here = slot == label
    place = jnp.broadcast_to(place_ref[...], (total, slots))
    caps = jnp.broadcast_to(cap_ref[...], (total, slots))
    place_c = jnp.sum(jnp.where(here, place, 0), axis=1, keepdims=True)
    cap_c = jnp.sum(jnp.where(here, caps, 0), axis=1, keepdims=True)
    same = place == place_c
    turn_c = jnp.sum(jnp.where(same & (slot < label), 1, 0), axis=1, keepdims=True)
    hosts_c = jnp.sum(jnp.where(same, 1, 0), axis=1, keepdims=True).astype(F32)
    used = jnp.zeros((total, toks), F32)
    weight = jnp.zeros((total, toks), F32)
    for k in range(top):
        pick = pick_ref[k : k + 1, :].astype(F32)
        wanted = pick - hosts_c * jnp.floor((pick + 0.5) / hosts_c)
        chosen = (ids_ref[k : k + 1, :] == place_c) & (wanted.astype(I32) == turn_c)
        used = jnp.where(chosen, 1.0, used)
        weight = jnp.where(chosen, gate_ref[k : k + 1, :], weight)
    earlier = lax.broadcasted_iota(I32, (toks, toks), 0) < lax.broadcasted_iota(I32, (toks, toks), 1)
    rank = jnp.dot(used, earlier.astype(F32), preferred_element_type=F32).astype(I32)
    seat = lax.broadcasted_iota(I32, (total, toks), 0) % cells
    spot = (used > 0.5) & (rank < cap_c) & (rank == seat)
    table = jnp.where(spot, weight, 0.0)
    block = 2 * cells
    width = rows_ref.shape[1]
    outs[-1][...] = table[: count * block]
    packed = jnp.dot(spot.astype(F32).astype(BF16), rows_ref[...], preferred_element_type=F32)
    for z, out in enumerate(outs[:-1]):
        part = slice(z * block, (z + 1) * block)
        out[:, :width] = packed[part].astype(BF16)
        if z >= count:
            lanes = out.shape[1] - width
            place = lax.broadcasted_iota(I32, (toks, lanes), 1) - lax.broadcasted_iota(I32, (toks, lanes), 0)
            tail = jnp.zeros((block, lanes), F32)
            for i, piece in enumerate(pieces(table[part])):
                shift = jnp.where(place == i * toks, 1.0, 0.0).astype(BF16)
                tail += jnp.dot(piece, shift, preferred_element_type=F32)
            out[:, width:] = tail.astype(BF16)


def split_kernel(cells, count, *refs):
    own_ref, oth_ref = refs[-2:]
    vals = [r[:, : own_ref.shape[1]].astype(F32) for r in refs[:count]]
    own_ref[...] = jnp.concatenate([v[:cells] for v in vals], axis=0).astype(BF16)
    oth_ref[...] = jnp.concatenate([v[cells:] for v in vals], axis=0).astype(BF16)


def join_kernel(count, *refs):
    refs[-1][...] = jnp.concatenate([r[...].astype(F32) for r in refs[:count]], axis=0).astype(BF16)


def half_kernel(keep_ref, core_ref, *refs):
    outs = refs[-4:]
    rows = outs[0].shape[0]
    for i, out in enumerate(outs):
        part = slice(i * rows, (i + 1) * rows)
        out[...] = (keep_ref[part, :] + core_ref[...].astype(F32)[part]).astype(out.dtype)


def lend_kernel(cells, keep_ref, core_ref, home_ref, *outs):
    total = keep_ref[...] + core_ref[...].astype(F32)
    rows = total.shape[0] // 4
    for z, out in enumerate((home_ref,) + outs):
        parts = [total[b * rows + z * cells : b * rows + (z + 1) * cells] for b in range(4)]
        out[...] = jnp.concatenate(parts, axis=0).astype(out.dtype)


def regroup_kernel(cells, count, *refs):
    vals = [r[...].astype(F32) for r in refs[:count]]
    for b, out in enumerate(refs[-4:]):
        out[...] = jnp.concatenate([v[b * cells : (b + 1) * cells] for v in vals], axis=0).astype(out.dtype)


def gathered(cells, count, own_ref, x_ref, y_ref, d_ref):
    own = own_ref[...] + x_ref[...].astype(F32)
    oth = y_ref[...].astype(F32) + d_ref[...].astype(F32)
    parts = [slice(z * cells, (z + 1) * cells) for z in range(count)]
    return [jnp.concatenate([own[p], oth[p]], axis=0).astype(BF16) for p in parts]


def weigh_kernel(cells, count, own_ref, x_ref, y_ref, d_ref, *refs):
    wides, outs = refs[:count], refs[-count:]
    width, toks = own_ref.shape[1], outs[0].shape[0]
    for z, rows in enumerate(gathered(cells, count, own_ref, x_ref, y_ref, d_ref)):
        total = None
        for i in range(3):
            w = lane_slice(wides[z][:, width:], i * toks, toks).astype(BF16)
            val = across(w, rows)
            total = val if total is None else total + val
        outs[z][...] = total.astype(outs[z].dtype)


def combine_kernel(cells, count, own_ref, x_ref, y_ref, d_ref, table_ref, top_ref, out_ref):
    rows = jnp.concatenate([v.astype(F32) for v in gathered(cells, count, own_ref, x_ref, y_ref, d_ref)], axis=0)
    total = top_ref[...].astype(F32)
    for piece in pieces(table_ref[...]):
        total += across(piece, rows.astype(BF16))
    out_ref[...] = total.astype(BF16)


def fetch_kernel(count, *refs):
    ins, outs, sem = refs[:count], refs[-count - 1 : -1], refs[-1]
    copies = [pltpu.make_async_copy(a, b, sem.at[i]) for i, (a, b) in enumerate(zip(ins, outs))]
    for c in copies:
        c.start()
    for c in copies:
        c.wait()


def up_kernel(near, far, *refs):
    rows, (gate_ref, up_ref), (far_hid, near_hid, acc_g, acc_u) = refs[:4], refs[4:6], refs[6:]
    acc_g[...] = jnp.zeros_like(acc_g)
    acc_u[...] = jnp.zeros_like(acc_u)

    def part(at, wat, step):
        x = jnp.concatenate([r[:, pl.ds(at, step)] for r in rows], axis=0)
        acc_g[...] += jnp.dot(x, gate_ref[pl.ds(wat, step), :], preferred_element_type=F32)
        acc_u[...] += jnp.dot(x, up_ref[pl.ds(wat, step), :], preferred_element_type=F32)

    sweep(part, 0, rows[0].shape[1], acc_g.shape[0] <= 256)
    g = acc_g[...]
    hid = (g / (1.0 + jnp.exp(-g)) * acc_u[...]).astype(BF16)
    far_hid[...] = hid[:far]
    near_hid[...] = hid[far:]


def down_kernel(hid_ref, down_ref, keep_ref, give_ref):
    rows = keep_ref.shape[0]

    def part(at, wat, step):
        val = jnp.dot(hid_ref[...], down_ref[:, pl.ds(wat, step)], preferred_element_type=F32)
        keep_ref[:, pl.ds(at, step)] = val[:rows]
        give_ref[:, pl.ds(at, step)] = val[rows:].astype(BF16)

    sweep(part, 0, keep_ref.shape[1], rows <= 128)


def per_device(
    hidden_in, expert_ids, gate_weights, replica_pick, placement, capacity, w_gate, w_up, w_down
):
    toks, width = hidden_in.shape
    top = expert_ids.shape[1]
    slots = placement.shape[0]
    devices = lax.axis_size("node")
    members = devices // slots
    cells = members * max(1, toks * top // (slots * members))
    high = slots // 2
    fw = w_gate.shape[1]
    my_slot = lax.axis_index("node") // members
    rows = high // 2 * cells
    any_ref = pl.BlockSpec(memory_space=pl.ANY)

    def send(value, flip):
        return lax.ppermute(value, "node", [(d, d ^ flip) for d in range(devices)])

    def over_z(block, z):
        return send(block, 2 * members * z)

    def split(blocks, when):
        return call(
            functools.partial(split_kernel, cells, len(blocks)),
            [shape((rows, width), BF16)] * 2,
            [VMEM] * len(blocks) + [any_ref] * len(when),
            "split",
        )(*blocks, *when)

    def fetch(arrays, when):
        return call(
            functools.partial(fetch_kernel, len(arrays)),
            [shape(w.shape, w.dtype) for w in arrays],
            [HBM] * len(arrays) + [any_ref] * len(when),
            "fetch",
            moved=sum(4 * w.size for w in arrays),
            limit=40,
            scratch=[pltpu.SemaphoreType.DMA((len(arrays),))],
        )(*arrays, *when)

    def spread(own, oth):
        d, y, x = send(oth, members + 2), send(oth, members), send(own, 2)
        return own, x, y, d

    def join(blocks, when):
        return call(
            functools.partial(join_kernel, 4),
            [shape((4 * rows, width), BF16)],
            [VMEM] * 4 + [any_ref] * len(when),
            "join",
        )(*blocks, *when)[0]

    half_z = high // 2
    block = 2 * cells
    lanes = -(-3 * toks // 128) * 128
    inputs = (expert_ids.T, gate_weights.T, replica_pick.T, placement[None, :], capacity[None, :], hidden_in)
    route = call(
        functools.partial(route_kernel, cells, half_z),
        [shape((block, width), BF16)] * half_z
        + [shape((block, width + lanes), BF16)] * half_z
        + [shape((half_z * block, toks), F32)],
        [SMEM] + [HBM] * 6,
        "route",
        limit=60,
        scratch=[pltpu.VMEM(a.shape, a.dtype) for a in inputs] + [pltpu.SemaphoreType.DMA((6,))],
    )(my_slot.reshape(1).astype(I32), *inputs)
    near_tab = route[-1]
    near_z = [over_z(route[z], z) for z in range(1, half_z)]
    far_wide = [over_z(route[z], z) for z in range(half_z, high)]
    (home,) = fetch([route[0]], ())
    near_own, near_oth = split([home] + near_z, ())
    near_got = spread(near_own, near_oth)
    (wg,) = fetch([w_gate], (near_own,))
    far_own, far_oth = split(far_wide, (wg,))
    far_got = spread(far_own, far_oth)
    near_all = join(near_got, (far_own,))
    near_core = send(near_all, 1)
    wu, wd = fetch([w_up, w_down], (near_all,))
    far_all = join(far_got, (wd,))
    far_core = send(far_all, 1)
    far_hid, near_hid, _, _ = call(
        functools.partial(up_kernel, 8 * rows, 8 * rows),
        [shape((8 * rows, fw), BF16)] * 2 + [shape((16 * rows, fw), F32)] * 2,
        [VMEM] * 6,
        "up",
        flops=64 * rows * fw * width,
    )(far_all, far_core, near_all, near_core, wg, wu)

    def down(hid, when):
        return call(
            down_kernel,
            [shape((4 * rows, width), F32), shape((4 * rows, width), BF16)],
            [VMEM] * 2 + [any_ref] * len(when),
            "down",
            flops=16 * rows * fw * width,
        )(hid, wd, *when)

    def half(keep, got, when):
        return call(
            half_kernel,
            [shape((rows, width), F32)] + [shape((rows, width), BF16)] * 3,
            [VMEM] * 2 + [any_ref] * len(when),
            "half",
        )(keep, got, *when)

    def gather(own, x, y, d):
        dg, yg, xg = send(d, members + 2), send(y, members), send(x, 2)
        return own, xg, yg, dg

    far_keep, far_give = down(far_hid, ())
    far_sib = send(far_give, 1)
    near_keep, near_give = down(near_hid, ())
    near_sib = send(near_give, 1)
    far_half = half(far_keep, far_sib, ())
    lent = call(
        functools.partial(lend_kernel, cells),
        [shape((4 * cells, width), F32)] + [shape((4 * cells, width), BF16)] * (half_z - 1),
        [VMEM] * 2,
        "lend",
    )(near_keep, near_sib)
    near_z = [lent[0]] + [over_z(lent[z], z) for z in range(1, half_z)]
    far_sum = call(
        functools.partial(weigh_kernel, cells, half_z),
        [shape((toks, width), F32)] + [shape((toks, width), BF16)] * (half_z - 1),
        [VMEM] * (4 + half_z),
        "weigh",
    )(*gather(*far_half), *far_wide)
    near_half = call(
        functools.partial(regroup_kernel, cells, half_z),
        [shape((rows, width), F32)] + [shape((rows, width), BF16)] * 3,
        [VMEM] * half_z + [any_ref],
        "regroup",
    )(*near_z, far_sum[0])
    top_sum = far_sum[0]
    for z in range(1, half_z):
        top_sum = top_sum + over_z(far_sum[z], z).astype(F32)
    top_back = over_z(top_sum.astype(BF16), half_z)
    (mixed,) = call(
        functools.partial(combine_kernel, cells, half_z),
        [shape((toks, width), BF16)],
        [VMEM] * 6,
        "combine",
    )(*gather(*near_half), near_tab, top_back)
    return mixed


def solution(mesh):
    split = P(("grp", "node"), None)
    placed = (split, split, split, split, P(), P(), P(None, "node"), P(None, "node"), P("node", None))
    return jax.shard_map(per_device, mesh=mesh, in_specs=placed, out_specs=split, check_vma=False)
```

```python
import functools

import jax
import jax.numpy as jnp
from jax import lax
from jax.experimental import pallas as pl
from jax.experimental.pallas import tpu as pltpu
from jax.sharding import PartitionSpec as P

BF16, F32, I32 = jnp.bfloat16, jnp.float32, jnp.int32
VMEM = pl.BlockSpec(memory_space=pltpu.VMEM)
SMEM = pl.BlockSpec(memory_space=pltpu.SMEM)
HBM = pl.BlockSpec(memory_space=pltpu.HBM)


def shape(dims, dtype):
    return jax.ShapeDtypeStruct(dims, dtype)


def call(kernel, outs, ins, name, flops=0, moved=0, limit=24, scratch=()):
    return pl.pallas_call(
        kernel,
        out_shape=outs,
        in_specs=ins,
        out_specs=[VMEM] * len(outs),
        scratch_shapes=list(scratch),
        compiler_params=pltpu.CompilerParams(vmem_limit_bytes=limit << 20),
        cost_estimate=pl.CostEstimate(flops=flops, bytes_accessed=moved, transcendentals=0),
        name=name,
    )


def pieces(weights):
    a = weights.astype(BF16)
    b = (weights - a.astype(F32)).astype(BF16)
    c = (weights - a.astype(F32) - b.astype(F32)).astype(BF16)
    return a, b, c


def across(left, right):
    return lax.dot_general(left, right, (((0,), (0,)), ((), ())), preferred_element_type=F32)


def sweep(part, base, width, unrolled):
    step = max(t for t in (1024, 896, 512, 256, 128) if width % t == 0)
    if unrolled:
        for at in range(0, width, step):
            part(at, base + at, step)
        return

    def body(i, unused):
        part(pl.multiple_of(i * step, 128), pl.multiple_of(base + i * step, 128), step)
        return unused

    lax.fori_loop(0, width // step, body, 0)


def route_kernel(cells, count, slot_ref, *refs):
    ins, outs, held, sem = refs[:6], refs[6:-7], refs[-7:-1], refs[-1]
    copies = [pltpu.make_async_copy(a, b, sem.at[i]) for i, (a, b) in enumerate(zip(ins, held))]
    for c in copies:
        c.start()
    for c in copies:
        c.wait()
    ids_ref, gate_ref, pick_ref, place_ref, cap_ref, rows_ref = held
    top, toks = ids_ref.shape
    slots = place_ref.shape[1]
    total = slots * cells
    cell = lax.broadcasted_iota(I32, (total, slots), 0)
    slot = lax.broadcasted_iota(I32, (total, slots), 1)
    label = jnp.bitwise_xor(cell // cells, slot_ref[0])
    here = slot == label
    place = jnp.broadcast_to(place_ref[...], (total, slots))
    caps = jnp.broadcast_to(cap_ref[...], (total, slots))
    place_c = jnp.sum(jnp.where(here, place, 0), axis=1, keepdims=True)
    cap_c = jnp.sum(jnp.where(here, caps, 0), axis=1, keepdims=True)
    same = place == place_c
    turn_c = jnp.sum(jnp.where(same & (slot < label), 1, 0), axis=1, keepdims=True)
    hosts_c = jnp.sum(jnp.where(same, 1, 0), axis=1, keepdims=True).astype(F32)
    used = jnp.zeros((total, toks), F32)
    weight = jnp.zeros((total, toks), F32)
    for k in range(top):
        pick = pick_ref[k : k + 1, :].astype(F32)
        wanted = pick - hosts_c * jnp.floor((pick + 0.5) / hosts_c)
        chosen = (ids_ref[k : k + 1, :] == place_c) & (wanted.astype(I32) == turn_c)
        used = jnp.where(chosen, 1.0, used)
        weight = jnp.where(chosen, gate_ref[k : k + 1, :], weight)
    earlier = lax.broadcasted_iota(I32, (toks, toks), 0) < lax.broadcasted_iota(I32, (toks, toks), 1)
    rank = jnp.dot(used, earlier.astype(F32), preferred_element_type=F32).astype(I32)
    seat = lax.broadcasted_iota(I32, (total, toks), 0) % cells
    spot = (used > 0.5) & (rank < cap_c) & (rank == seat)
    table = jnp.where(spot, weight, 0.0)
    block = 2 * cells
    width = rows_ref.shape[1]
    n = count * block
    eye = jnp.where(lax.broadcasted_iota(I32, (n, n), 0) == lax.broadcasted_iota(I32, (n, n), 1), 1.0, 0.0).astype(BF16)
    outs[-1][...] = jnp.concatenate([across(piece, eye) for piece in pieces(table[:n])], axis=0)
    packed = jnp.dot(spot.astype(F32).astype(BF16), rows_ref[...], preferred_element_type=F32)
    for z, out in enumerate(outs[:-1]):
        part = slice(z * block, (z + 1) * block)
        out[:, :width] = packed[part].astype(BF16)
        if z >= count:
            lanes = out.shape[1] - width
            place = lax.broadcasted_iota(I32, (toks, lanes), 1) - lax.broadcasted_iota(I32, (toks, lanes), 0)
            tail = jnp.zeros((block, lanes), F32)
            for i, piece in enumerate(pieces(table[part])):
                shift = jnp.where(place == i * toks, 1.0, 0.0).astype(BF16)
                tail += jnp.dot(piece, shift, preferred_element_type=F32)
            out[:, width:] = tail.astype(BF16)


def split_kernel(cells, count, *refs):
    own_ref, oth_ref = refs[-2:]
    vals = [r[:, : own_ref.shape[1]].astype(F32) for r in refs[:count]]
    own_ref[...] = jnp.concatenate([v[:cells] for v in vals], axis=0).astype(BF16)
    oth_ref[...] = jnp.concatenate([v[cells:] for v in vals], axis=0).astype(BF16)


def join_kernel(count, *refs):
    refs[-1][...] = jnp.concatenate([r[...].astype(F32) for r in refs[:count]], axis=0).astype(BF16)


def half_kernel(keep_ref, core_ref, *refs):
    outs = refs[-4:]
    rows = outs[0].shape[0]
    for i, out in enumerate(outs):
        part = slice(i * rows, (i + 1) * rows)
        out[...] = (keep_ref[part, :] + core_ref[...].astype(F32)[part]).astype(out.dtype)


def lend_kernel(cells, keep_ref, core_ref, home_ref, *outs):
    total = keep_ref[...] + core_ref[...].astype(F32)
    rows = total.shape[0] // 4
    for z, out in enumerate((home_ref,) + outs):
        parts = [total[b * rows + z * cells : b * rows + (z + 1) * cells] for b in range(4)]
        out[...] = jnp.concatenate(parts, axis=0).astype(out.dtype)


def regroup_kernel(cells, count, *refs):
    vals = [r[...].astype(F32) for r in refs[:count]]
    for b, out in enumerate(refs[-4:]):
        out[...] = jnp.concatenate([v[b * cells : (b + 1) * cells] for v in vals], axis=0).astype(out.dtype)


def weighted(weights, groups):
    rows = jnp.concatenate([g.astype(F32) for g in groups], axis=0).astype(BF16)
    return jnp.dot(weights.astype(BF16), rows, preferred_element_type=F32)


def gathered(cells, count, own_ref, x_ref, y_ref, d_ref):
    own = own_ref[...] + x_ref[...].astype(F32)
    oth = y_ref[...].astype(F32) + d_ref[...].astype(F32)
    parts = [slice(z * cells, (z + 1) * cells) for z in range(count)]
    return [jnp.concatenate([own[p], oth[p]], axis=0).astype(BF16) for p in parts]


def weigh_kernel(cells, count, own_ref, x_ref, y_ref, d_ref, *refs):
    wides, outs = refs[:count], refs[-count:]
    width, toks, block = own_ref.shape[1], outs[0].shape[0], 2 * cells
    left = []
    for z, wide in enumerate(wides):
        place = lax.broadcasted_iota(I32, (block, count * block), 1) - lax.broadcasted_iota(I32, (block, count * block), 0)
        shift = jnp.where(place == z * block, 1.0, 0.0).astype(BF16)
        left.append(across(wide[:, width:], shift)[: 3 * toks])
    val = weighted(jnp.concatenate(left, axis=0), gathered(cells, count, own_ref, x_ref, y_ref, d_ref))
    for z, out in enumerate(outs):
        a, b, c = (val[(3 * z + i) * toks : (3 * z + i + 1) * toks] for i in range(3))
        out[...] = (a + b + c).astype(out.dtype)


def combine_kernel(cells, count, own_ref, x_ref, y_ref, d_ref, table_ref, top_ref, out_ref):
    toks = out_ref.shape[0]
    val = weighted(table_ref[...], gathered(cells, count, own_ref, x_ref, y_ref, d_ref))
    total = val[:toks] + val[toks : 2 * toks] + val[2 * toks :]
    out_ref[...] = (total + top_ref[...].astype(F32)).astype(BF16)


def fetch_kernel(count, *refs):
    ins, outs, sem = refs[:count], refs[-count - 1 : -1], refs[-1]
    copies = [pltpu.make_async_copy(a, b, sem.at[i]) for i, (a, b) in enumerate(zip(ins, outs))]
    for c in copies:
        c.start()
    for c in copies:
        c.wait()


def up_kernel(near, far, *refs):
    rows, (gate_ref, up_ref), (far_hid, near_hid, acc_g, acc_u) = refs[:4], refs[4:6], refs[6:]
    acc_g[...] = jnp.zeros_like(acc_g)
    acc_u[...] = jnp.zeros_like(acc_u)

    def part(at, wat, step):
        x = jnp.concatenate([r[:, pl.ds(at, step)] for r in rows], axis=0)
        acc_g[...] += jnp.dot(x, gate_ref[pl.ds(wat, step), :], preferred_element_type=F32)
        acc_u[...] += jnp.dot(x, up_ref[pl.ds(wat, step), :], preferred_element_type=F32)

    sweep(part, 0, rows[0].shape[1], acc_g.shape[0] <= 256)
    g = acc_g[...]
    hid = (g / (1.0 + jnp.exp(-g)) * acc_u[...]).astype(BF16)
    far_hid[...] = hid[:far]
    near_hid[...] = hid[far:]


def down_kernel(hid_ref, down_ref, keep_ref, give_ref):
    rows = keep_ref.shape[0]

    def part(at, wat, step):
        val = jnp.dot(hid_ref[...], down_ref[:, pl.ds(wat, step)], preferred_element_type=F32)
        keep_ref[:, pl.ds(at, step)] = val[:rows]
        give_ref[:, pl.ds(at, step)] = val[rows:].astype(BF16)

    sweep(part, 0, keep_ref.shape[1], rows <= 128)


def per_device(
    hidden_in, expert_ids, gate_weights, replica_pick, placement, capacity, w_gate, w_up, w_down
):
    toks, width = hidden_in.shape
    top = expert_ids.shape[1]
    slots = placement.shape[0]
    devices = lax.axis_size("node")
    members = devices // slots
    cells = members * max(1, toks * top // (slots * members))
    high = slots // 2
    fw = w_gate.shape[1]
    my_slot = lax.axis_index("node") // members
    rows = high // 2 * cells
    any_ref = pl.BlockSpec(memory_space=pl.ANY)

    def send(value, flip):
        return lax.ppermute(value, "node", [(d, d ^ flip) for d in range(devices)])

    def over_z(block, z):
        return send(block, 2 * members * z)

    def split(blocks, when):
        return call(
            functools.partial(split_kernel, cells, len(blocks)),
            [shape((rows, width), BF16)] * 2,
            [VMEM] * len(blocks) + [any_ref] * len(when),
            "split",
        )(*blocks, *when)

    def fetch(arrays, when):
        return call(
            functools.partial(fetch_kernel, len(arrays)),
            [shape(w.shape, w.dtype) for w in arrays],
            [HBM] * len(arrays) + [any_ref] * len(when),
            "fetch",
            moved=sum(4 * w.size for w in arrays),
            limit=40,
            scratch=[pltpu.SemaphoreType.DMA((len(arrays),))],
        )(*arrays, *when)

    def spread(own, oth):
        d, y, x = send(oth, members + 2), send(oth, members), send(own, 2)
        return own, x, y, d

    def join(blocks, when):
        return call(
            functools.partial(join_kernel, 4),
            [shape((4 * rows, width), BF16)],
            [VMEM] * 4 + [any_ref] * len(when),
            "join",
        )(*blocks, *when)[0]

    half_z = high // 2
    block = 2 * cells
    lanes = -(-3 * toks // 128) * 128
    inputs = (expert_ids.T, gate_weights.T, replica_pick.T, placement[None, :], capacity[None, :], hidden_in)
    route = call(
        functools.partial(route_kernel, cells, half_z),
        [shape((block, width), BF16)] * half_z
        + [shape((block, width + lanes), BF16)] * half_z
        + [shape((3 * toks, half_z * block), F32)],
        [SMEM] + [HBM] * 6,
        "route",
        limit=60,
        scratch=[pltpu.VMEM(a.shape, a.dtype) for a in inputs] + [pltpu.SemaphoreType.DMA((6,))],
    )(my_slot.reshape(1).astype(I32), *inputs)
    near_tab = route[-1]
    near_z = [over_z(route[z], z) for z in range(1, half_z)]
    far_wide = [over_z(route[z], z) for z in range(half_z, high)]
    (home,) = fetch([route[0]], ())
    near_own, near_oth = split([home] + near_z, ())
    near_got = spread(near_own, near_oth)
    (wg,) = fetch([w_gate], (near_own,))
    far_own, far_oth = split(far_wide, (wg,))
    far_got = spread(far_own, far_oth)
    near_all = join(near_got, (far_own,))
    near_core = send(near_all, 1)
    wu, wd = fetch([w_up, w_down], (near_all,))
    far_all = join(far_got, (wd,))
    far_core = send(far_all, 1)
    far_hid, near_hid, _, _ = call(
        functools.partial(up_kernel, 8 * rows, 8 * rows),
        [shape((8 * rows, fw), BF16)] * 2 + [shape((16 * rows, fw), F32)] * 2,
        [VMEM] * 6,
        "up",
        flops=64 * rows * fw * width,
    )(far_all, far_core, near_all, near_core, wg, wu)

    def down(hid, when):
        return call(
            down_kernel,
            [shape((4 * rows, width), F32), shape((4 * rows, width), BF16)],
            [VMEM] * 2 + [any_ref] * len(when),
            "down",
            flops=16 * rows * fw * width,
        )(hid, wd, *when)

    def half(keep, got, when):
        return call(
            half_kernel,
            [shape((rows, width), F32)] + [shape((rows, width), BF16)] * 3,
            [VMEM] * 2 + [any_ref] * len(when),
            "half",
        )(keep, got, *when)

    def gather(own, x, y, d):
        dg, yg, xg = send(d, members + 2), send(y, members), send(x, 2)
        return own, xg, yg, dg

    far_keep, far_give = down(far_hid, ())
    far_sib = send(far_give, 1)
    near_keep, near_give = down(near_hid, ())
    near_sib = send(near_give, 1)
    far_half = half(far_keep, far_sib, ())
    lent = call(
        functools.partial(lend_kernel, cells),
        [shape((4 * cells, width), F32)] + [shape((4 * cells, width), BF16)] * (half_z - 1),
        [VMEM] * 2,
        "lend",
    )(near_keep, near_sib)
    near_z = [lent[0]] + [over_z(lent[z], z) for z in range(1, half_z)]
    far_sum = call(
        functools.partial(weigh_kernel, cells, half_z),
        [shape((toks, width), F32)] + [shape((toks, width), BF16)] * (half_z - 1),
        [VMEM] * (4 + half_z),
        "weigh",
    )(*gather(*far_half), *far_wide)
    near_half = call(
        functools.partial(regroup_kernel, cells, half_z),
        [shape((rows, width), F32)] + [shape((rows, width), BF16)] * 3,
        [VMEM] * half_z + [any_ref],
        "regroup",
    )(*near_z, far_sum[0])
    top_sum = far_sum[0]
    for z in range(1, half_z):
        top_sum = top_sum + over_z(far_sum[z], z).astype(F32)
    top_back = over_z(top_sum.astype(BF16), half_z)
    (mixed,) = call(
        functools.partial(combine_kernel, cells, half_z),
        [shape((toks, width), BF16)],
        [VMEM] * 6,
        "combine",
    )(*gather(*near_half), near_tab, top_back)
    return mixed


def solution(mesh):
    split = P(("grp", "node"), None)
    placed = (split, split, split, split, P(), P(), P(None, "node"), P(None, "node"), P("node", None))
    return jax.shard_map(per_device, mesh=mesh, in_specs=placed, out_specs=split, check_vma=False)
```

```python
import functools

import jax
import jax.numpy as jnp
from jax import lax
from jax.experimental import pallas as pl
from jax.experimental.pallas import tpu as pltpu
from jax.sharding import PartitionSpec as P

BF16, F32, I32 = jnp.bfloat16, jnp.float32, jnp.int32
VMEM = pl.BlockSpec(memory_space=pltpu.VMEM)
SMEM = pl.BlockSpec(memory_space=pltpu.SMEM)
HBM = pl.BlockSpec(memory_space=pltpu.HBM)


def shape(dims, dtype):
    return jax.ShapeDtypeStruct(dims, dtype)


def call(kernel, outs, ins, name, flops=0, moved=0, limit=24, scratch=(), out=VMEM):
    return pl.pallas_call(
        kernel,
        out_shape=outs,
        in_specs=ins,
        out_specs=[out] * len(outs),
        scratch_shapes=list(scratch),
        compiler_params=pltpu.CompilerParams(vmem_limit_bytes=limit << 20),
        cost_estimate=pl.CostEstimate(flops=flops, bytes_accessed=moved, transcendentals=0),
        name=name,
    )


def pieces(weights):
    a = weights.astype(BF16)
    b = (weights - a.astype(F32)).astype(BF16)
    c = (weights - a.astype(F32) - b.astype(F32)).astype(BF16)
    return a, b, c


def across(left, right):
    return lax.dot_general(left, right, (((0,), (0,)), ((), ())), preferred_element_type=F32)


def sweep(part, base, width, unrolled):
    step = max(t for t in (1024, 896, 512, 256, 128) if width % t == 0)
    if unrolled:
        for at in range(0, width, step):
            part(at, base + at, step)
        return

    def body(i, unused):
        part(pl.multiple_of(i * step, 128), pl.multiple_of(base + i * step, 128), step)
        return unused

    lax.fori_loop(0, width // step, body, 0)


def route_kernel(cells, count, slot_ref, *refs):
    ins, held, sems = refs[:6], refs[-8:-2], refs[-2:]
    dests, outs = refs[6 : 6 + (len(refs) - 14) // 2], refs[6 + (len(refs) - 14) // 2 : -8]
    copies = [pltpu.make_async_copy(a, b, sems[0].at[i]) for i, (a, b) in enumerate(zip(ins, held))]
    for c in copies:
        c.start()
    for c in copies[:-1]:
        c.wait()
    ids_ref, gate_ref, pick_ref, place_ref, cap_ref, rows_ref = held
    top, toks = ids_ref.shape
    slots = place_ref.shape[1]
    total = slots * cells
    cell = lax.broadcasted_iota(I32, (total, slots), 0)
    slot = lax.broadcasted_iota(I32, (total, slots), 1)
    label = jnp.bitwise_xor(cell // cells, slot_ref[0])
    here = slot == label
    place = jnp.broadcast_to(place_ref[...], (total, slots))
    caps = jnp.broadcast_to(cap_ref[...], (total, slots))
    place_c = jnp.sum(jnp.where(here, place, 0), axis=1, keepdims=True)
    cap_c = jnp.sum(jnp.where(here, caps, 0), axis=1, keepdims=True)
    same = place == place_c
    turn_c = jnp.sum(jnp.where(same & (slot < label), 1, 0), axis=1, keepdims=True)
    hosts_c = jnp.sum(jnp.where(same, 1, 0), axis=1, keepdims=True).astype(F32)
    used = jnp.zeros((total, toks), F32)
    weight = jnp.zeros((total, toks), F32)
    for k in range(top):
        pick = pick_ref[k : k + 1, :].astype(F32)
        wanted = pick - hosts_c * jnp.floor((pick + 0.5) / hosts_c)
        chosen = (ids_ref[k : k + 1, :] == place_c) & (wanted.astype(I32) == turn_c)
        used = jnp.where(chosen, 1.0, used)
        weight = jnp.where(chosen, gate_ref[k : k + 1, :], weight)
    earlier = lax.broadcasted_iota(I32, (toks, toks), 0) < lax.broadcasted_iota(I32, (toks, toks), 1)
    rank = jnp.dot(used, earlier.astype(F32), preferred_element_type=F32).astype(I32)
    seat = lax.broadcasted_iota(I32, (total, toks), 0) % cells
    spot = (used > 0.5) & (rank < cap_c) & (rank == seat)
    table = jnp.where(spot, weight, 0.0)
    block = 2 * cells
    width = rows_ref.shape[1]
    n = count * block
    eye = jnp.where(lax.broadcasted_iota(I32, (n, n), 0) == lax.broadcasted_iota(I32, (n, n), 1), 1.0, 0.0).astype(BF16)
    outs[-1][...] = jnp.concatenate([across(piece, eye) for piece in pieces(table[:n])], axis=0)
    for z, out in enumerate(outs[:-1]):
        part = slice(z * block, (z + 1) * block)
        if z >= count:
            lanes = out.shape[1] - width
            place = lax.broadcasted_iota(I32, (toks, lanes), 1) - lax.broadcasted_iota(I32, (toks, lanes), 0)
            tail = jnp.zeros((block, lanes), F32)
            for i, piece in enumerate(pieces(table[part])):
                shift = jnp.where(place == i * toks, 1.0, 0.0).astype(BF16)
                tail += jnp.dot(piece, shift, preferred_element_type=F32)
            out[:, width:] = tail.astype(BF16)
    copies[-1].wait()
    pack = spot.astype(F32).astype(BF16)
    back = [pltpu.make_async_copy(a, b, sems[1].at[i]) for i, (a, b) in enumerate(zip(outs, dests))]
    back[-1].start()
    packed = jnp.dot(pack, rows_ref[...], preferred_element_type=F32)
    for z, out in enumerate(outs[:-1]):
        out[:, :width] = packed[z * block : (z + 1) * block].astype(BF16)
        back[z].start()
    for c in back:
        c.wait()


def split_kernel(cells, count, *refs):
    own_ref, oth_ref = refs[-2:]
    vals = [r[:, : own_ref.shape[1]].astype(F32) for r in refs[:count]]
    own_ref[...] = jnp.concatenate([v[:cells] for v in vals], axis=0).astype(BF16)
    oth_ref[...] = jnp.concatenate([v[cells:] for v in vals], axis=0).astype(BF16)


def join_kernel(count, *refs):
    refs[-1][...] = jnp.concatenate([r[...].astype(F32) for r in refs[:count]], axis=0).astype(BF16)


def half_kernel(keep_ref, core_ref, *refs):
    outs = refs[-4:]
    rows = outs[0].shape[0]
    for i, out in enumerate(outs):
        part = slice(i * rows, (i + 1) * rows)
        out[...] = (keep_ref[part, :] + core_ref[...].astype(F32)[part]).astype(out.dtype)


def lend_kernel(cells, keep_ref, core_ref, home_ref, *outs):
    total = keep_ref[...] + core_ref[...].astype(F32)
    rows = total.shape[0] // 4
    for i, out in enumerate((home_ref,) + outs):
        z, blocks = (0, range(4)) if i == 0 else ((i + 1) // 2, ((0, 1), (2, 3))[(i - 1) % 2])
        parts = [total[b * rows + z * cells : b * rows + (z + 1) * cells] for b in blocks]
        out[...] = jnp.concatenate(parts, axis=0).astype(out.dtype)


def regroup_kernel(cells, count, *refs):
    ins = [r[...].astype(F32) for r in refs[: 2 * count - 1]]
    vals = ins[:1] + [jnp.concatenate(ins[i : i + 2], axis=0) for i in range(1, 2 * count - 1, 2)]
    for b, out in enumerate(refs[-4:]):
        out[...] = jnp.concatenate([v[b * cells : (b + 1) * cells] for v in vals], axis=0).astype(out.dtype)


def weighted(weights, groups):
    rows = jnp.concatenate([g.astype(F32) for g in groups], axis=0).astype(BF16)
    return jnp.dot(weights.astype(BF16), rows, preferred_element_type=F32)


def gathered(cells, count, own_ref, x_ref, y_ref, d_ref):
    own = own_ref[...] + x_ref[...].astype(F32)
    oth = y_ref[...].astype(F32) + d_ref[...].astype(F32)
    parts = [slice(z * cells, (z + 1) * cells) for z in range(count)]
    return [jnp.concatenate([own[p], oth[p]], axis=0).astype(BF16) for p in parts]


def weigh_kernel(cells, count, own_ref, x_ref, y_ref, d_ref, *refs):
    wides, outs = refs[:count], refs[-count:]
    width, toks, block = own_ref.shape[1], outs[0].shape[0], 2 * cells
    left = []
    for z, wide in enumerate(wides):
        place = lax.broadcasted_iota(I32, (block, count * block), 1) - lax.broadcasted_iota(I32, (block, count * block), 0)
        shift = jnp.where(place == z * block, 1.0, 0.0).astype(BF16)
        left.append(across(wide[:, width:], shift)[: 3 * toks])
    val = weighted(jnp.concatenate(left, axis=0), gathered(cells, count, own_ref, x_ref, y_ref, d_ref))
    for z, out in enumerate(outs):
        a, b, c = (val[(3 * z + i) * toks : (3 * z + i + 1) * toks] for i in range(3))
        out[...] = (a + b + c).astype(out.dtype)


def combine_kernel(cells, count, own_ref, x_ref, y_ref, d_ref, table_ref, top_ref, out_ref):
    toks = out_ref.shape[0]
    val = weighted(table_ref[...], gathered(cells, count, own_ref, x_ref, y_ref, d_ref))
    total = val[:toks] + val[toks : 2 * toks] + val[2 * toks :]
    out_ref[...] = (total + top_ref[...].astype(F32)).astype(BF16)


def fetch_kernel(count, *refs):
    ins, outs, sem = refs[:count], refs[-count - 1 : -1], refs[-1]
    copies = [pltpu.make_async_copy(a, b, sem.at[i]) for i, (a, b) in enumerate(zip(ins, outs))]
    for c in copies:
        c.start()
    for c in copies:
        c.wait()


def up_kernel(near, far, *refs):
    rows, (gate_ref, up_ref), (far_hid, near_hid, acc_g, acc_u) = refs[:4], refs[4:6], refs[6:]
    acc_g[...] = jnp.zeros_like(acc_g)
    acc_u[...] = jnp.zeros_like(acc_u)

    def part(at, wat, step):
        x = jnp.concatenate([r[:, pl.ds(at, step)] for r in rows], axis=0)
        acc_g[...] += jnp.dot(x, gate_ref[pl.ds(wat, step), :], preferred_element_type=F32)
        acc_u[...] += jnp.dot(x, up_ref[pl.ds(wat, step), :], preferred_element_type=F32)

    sweep(part, 0, rows[0].shape[1], acc_g.shape[0] <= 256)
    g = acc_g[...]
    hid = (g / (1.0 + jnp.exp(-g)) * acc_u[...]).astype(BF16)
    far_hid[...] = hid[:far]
    near_hid[...] = hid[far:]


def down_kernel(far_ref, near_ref, down_ref, *outs):
    hid = jnp.concatenate([far_ref[...], near_ref[...]], axis=0)
    rows = outs[0].shape[0]

    def part(at, wat, step):
        val = jnp.dot(hid, down_ref[:, pl.ds(wat, step)], preferred_element_type=F32)
        for i, out in enumerate(outs):
            out[:, pl.ds(at, step)] = val[i * rows : (i + 1) * rows].astype(out.dtype)

    sweep(part, 0, outs[0].shape[1], rows <= 128)


def per_device(
    hidden_in, expert_ids, gate_weights, replica_pick, placement, capacity, w_gate, w_up, w_down
):
    toks, width = hidden_in.shape
    top = expert_ids.shape[1]
    slots = placement.shape[0]
    devices = lax.axis_size("node")
    members = devices // slots
    cells = members * max(1, toks * top // (slots * members))
    high = slots // 2
    fw = w_gate.shape[1]
    my_slot = lax.axis_index("node") // members
    rows = high // 2 * cells
    any_ref = pl.BlockSpec(memory_space=pl.ANY)

    def send(value, flip):
        return lax.ppermute(value, "node", [(d, d ^ flip) for d in range(devices)])

    def over_z(block, z):
        return send(block, 2 * members * z)

    def split(blocks, when):
        return call(
            functools.partial(split_kernel, cells, len(blocks)),
            [shape((rows, width), BF16)] * 2,
            [VMEM] * len(blocks) + [any_ref] * len(when),
            "split",
        )(*blocks, *when)

    def fetch(arrays, when):
        return call(
            functools.partial(fetch_kernel, len(arrays)),
            [shape(w.shape, w.dtype) for w in arrays],
            [HBM] * len(arrays) + [any_ref] * len(when),
            "fetch",
            moved=sum(4 * w.size for w in arrays),
            limit=40,
            scratch=[pltpu.SemaphoreType.DMA((len(arrays),))],
        )(*arrays, *when)

    def spread(own, oth):
        d, y, x = send(oth, members + 2), send(oth, members), send(own, 2)
        return own, x, y, d

    def join(blocks, when):
        return call(
            functools.partial(join_kernel, 4),
            [shape((4 * rows, width), BF16)],
            [VMEM] * 4 + [any_ref] * len(when),
            "join",
        )(*blocks, *when)[0]

    half_z = high // 2
    block = 2 * cells
    lanes = -(-3 * toks // 128) * 128
    inputs = (expert_ids.T, gate_weights.T, replica_pick.T, placement[None, :], capacity[None, :], hidden_in)
    made = (
        [shape((block, width), BF16)] * half_z
        + [shape((block, width + lanes), BF16)] * half_z
        + [shape((3 * toks, half_z * block), F32)]
    )
    route = call(
        functools.partial(route_kernel, cells, half_z),
        made,
        [SMEM] + [HBM] * 6,
        "route",
        limit=60,
        scratch=[pltpu.VMEM(a.shape, a.dtype) for a in made]
        + [pltpu.VMEM(a.shape, a.dtype) for a in inputs]
        + [pltpu.SemaphoreType.DMA((6,)), pltpu.SemaphoreType.DMA((len(made),))],
        out=HBM,
    )(my_slot.reshape(1).astype(I32), *inputs)
    near_tab = route[-1]
    near_z = [over_z(route[z], z) for z in range(1, half_z)]
    far_wide = [over_z(route[z], z) for z in range(half_z, high)]
    (home,) = fetch([route[0]], ())
    near_own, near_oth = split([home] + near_z, ())
    near_got = spread(near_own, near_oth)
    (wg,) = fetch([w_gate], (near_own,))
    far_own, far_oth = split(far_wide, (wg,))
    far_got = spread(far_own, far_oth)
    near_all = join(near_got, (far_own,))
    near_core = send(near_all, 1)
    wu, wd = fetch([w_up, w_down], (near_all,))
    far_all = join(far_got, (wd,))
    far_core = send(far_all, 1)
    far_hid, near_hid, _, _ = call(
        functools.partial(up_kernel, 8 * rows, 8 * rows),
        [shape((8 * rows, fw), BF16)] * 2 + [shape((16 * rows, fw), F32)] * 2,
        [VMEM] * 6,
        "up",
        flops=64 * rows * fw * width,
    )(far_all, far_core, near_all, near_core, wg, wu)

    def half(keep, got, when):
        return call(
            half_kernel,
            [shape((rows, width), F32)] + [shape((rows, width), BF16)] * 3,
            [VMEM] * 2 + [any_ref] * len(when),
            "half",
        )(keep, got, *when)

    def gather(own, x, y, d):
        dg, yg, xg = send(d, members + 2), send(y, members), send(x, 2)
        return own, xg, yg, dg

    far_keep, far_give, near_keep, near_give = call(
        down_kernel,
        [shape((4 * rows, width), F32), shape((4 * rows, width), BF16)] * 2,
        [VMEM] * 3,
        "down",
        flops=32 * rows * fw * width,
    )(far_hid, near_hid, wd)
    far_sib = send(far_give, 1)
    near_sib = send(near_give, 1)
    far_half = half(far_keep, far_sib, ())
    lent = call(
        functools.partial(lend_kernel, cells),
        [shape((4 * cells, width), F32)] + [shape((2 * cells, width), BF16)] * (2 * half_z - 2),
        [VMEM] * 2,
        "lend",
    )(near_keep, near_sib)
    near_z = [lent[0]] + [over_z(lent[i], (i + 1) // 2) for i in range(1, 2 * half_z - 1)]
    far_sum = call(
        functools.partial(weigh_kernel, cells, half_z),
        [shape((toks, width), F32)] + [shape((toks, width), BF16)] * (half_z - 1),
        [VMEM] * (4 + half_z),
        "weigh",
    )(*gather(*far_half), *far_wide)
    near_half = call(
        functools.partial(regroup_kernel, cells, half_z),
        [shape((rows, width), F32)] + [shape((rows, width), BF16)] * 3,
        [VMEM] * (2 * half_z - 1) + [any_ref],
        "regroup",
    )(*near_z, far_sum[0])
    top_sum = far_sum[0]
    for z in range(1, half_z):
        top_sum = top_sum + over_z(far_sum[z], z).astype(F32)
    top_back = over_z(top_sum.astype(BF16), half_z)
    (mixed,) = call(
        functools.partial(combine_kernel, cells, half_z),
        [shape((toks, width), BF16)],
        [VMEM] * 6,
        "combine",
    )(*gather(*near_half), near_tab, top_back)
    return mixed


def solution(mesh):
    split = P(("grp", "node"), None)
    placed = (split, split, split, split, P(), P(), P(None, "node"), P(None, "node"), P("node", None))
    return jax.shard_map(per_device, mesh=mesh, in_specs=placed, out_specs=split, check_vma=False)
```

```python
import functools

import jax
import jax.numpy as jnp
from jax import lax
from jax.experimental import pallas as pl
from jax.experimental.pallas import tpu as pltpu
from jax.sharding import PartitionSpec as P

BF16, F32, I32 = jnp.bfloat16, jnp.float32, jnp.int32
VMEM = pl.BlockSpec(memory_space=pltpu.VMEM)
SMEM = pl.BlockSpec(memory_space=pltpu.SMEM)
HBM = pl.BlockSpec(memory_space=pltpu.HBM)


def shape(dims, dtype):
    return jax.ShapeDtypeStruct(dims, dtype)


def call(kernel, outs, ins, name, flops=0, moved=0, limit=24, scratch=(), out=VMEM):
    return pl.pallas_call(
        kernel,
        out_shape=outs,
        in_specs=ins,
        out_specs=[out] * len(outs),
        scratch_shapes=list(scratch),
        compiler_params=pltpu.CompilerParams(vmem_limit_bytes=limit << 20),
        cost_estimate=pl.CostEstimate(flops=flops, bytes_accessed=moved, transcendentals=0),
        name=name,
    )


def pieces(weights):
    a = weights.astype(BF16)
    b = (weights - a.astype(F32)).astype(BF16)
    c = (weights - a.astype(F32) - b.astype(F32)).astype(BF16)
    return a, b, c


def across(left, right):
    return lax.dot_general(left, right, (((0,), (0,)), ((), ())), preferred_element_type=F32)


def sweep(part, base, width, unrolled):
    step = max(t for t in (1024, 896, 512, 256, 128) if width % t == 0)
    if unrolled:
        for at in range(0, width, step):
            part(at, base + at, step)
        return

    def body(i, unused):
        part(pl.multiple_of(i * step, 128), pl.multiple_of(base + i * step, 128), step)
        return unused

    lax.fori_loop(0, width // step, body, 0)


def route_kernel(cells, count, slot_ref, *refs):
    ins, held, sems = refs[:6], refs[-8:-2], refs[-2:]
    dests, outs = refs[6 : 6 + (len(refs) - 14) // 2], refs[6 + (len(refs) - 14) // 2 : -8]
    copies = [pltpu.make_async_copy(a, b, sems[0].at[i]) for i, (a, b) in enumerate(zip(ins, held))]
    for c in copies:
        c.start()
    for c in copies[:-1]:
        c.wait()
    ids_ref, gate_ref, pick_ref, place_ref, cap_ref, rows_ref = held
    top, toks = ids_ref.shape
    slots = place_ref.shape[1]
    total = slots * cells
    cell = lax.broadcasted_iota(I32, (total, slots), 0)
    slot = lax.broadcasted_iota(I32, (total, slots), 1)
    label = jnp.bitwise_xor(cell // cells, slot_ref[0])
    here = slot == label
    place = jnp.broadcast_to(place_ref[...], (total, slots))
    caps = jnp.broadcast_to(cap_ref[...], (total, slots))
    place_c = jnp.sum(jnp.where(here, place, 0), axis=1, keepdims=True)
    cap_c = jnp.sum(jnp.where(here, caps, 0), axis=1, keepdims=True)
    same = place == place_c
    turn_c = jnp.sum(jnp.where(same & (slot < label), 1, 0), axis=1, keepdims=True)
    hosts_c = jnp.sum(jnp.where(same, 1, 0), axis=1, keepdims=True).astype(F32)
    used = jnp.zeros((total, toks), F32)
    weight = jnp.zeros((total, toks), F32)
    for k in range(top):
        pick = pick_ref[k : k + 1, :].astype(F32)
        wanted = pick - hosts_c * jnp.floor((pick + 0.5) / hosts_c)
        chosen = (ids_ref[k : k + 1, :] == place_c) & (wanted.astype(I32) == turn_c)
        used = jnp.where(chosen, 1.0, used)
        weight = jnp.where(chosen, gate_ref[k : k + 1, :], weight)
    earlier = lax.broadcasted_iota(I32, (toks, toks), 0) < lax.broadcasted_iota(I32, (toks, toks), 1)
    rank = jnp.dot(used, earlier.astype(F32), preferred_element_type=F32).astype(I32)
    seat = lax.broadcasted_iota(I32, (total, toks), 0) % cells
    spot = (used > 0.5) & (rank < cap_c) & (rank == seat)
    table = jnp.where(spot, weight, 0.0)
    block = 2 * cells
    width = rows_ref.shape[1]
    n = count * block
    eye = jnp.where(lax.broadcasted_iota(I32, (n, n), 0) == lax.broadcasted_iota(I32, (n, n), 1), 1.0, 0.0).astype(BF16)
    outs[-1][...] = jnp.concatenate([across(piece, eye) for piece in pieces(table[:n])], axis=0)
    for z, out in enumerate(outs[:-1]):
        part = slice(z * block, (z + 1) * block)
        if z >= count:
            lanes = out.shape[1] - width
            place = lax.broadcasted_iota(I32, (toks, lanes), 1) - lax.broadcasted_iota(I32, (toks, lanes), 0)
            tail = jnp.zeros((block, lanes), F32)
            for i, piece in enumerate(pieces(table[part])):
                shift = jnp.where(place == i * toks, 1.0, 0.0).astype(BF16)
                tail += jnp.dot(piece, shift, preferred_element_type=F32)
            out[:, width:] = tail.astype(BF16)
    copies[-1].wait()
    pack = spot.astype(F32).astype(BF16)
    back = [pltpu.make_async_copy(a, b, sems[1].at[i]) for i, (a, b) in enumerate(zip(outs, dests))]
    back[-1].start()
    packed = jnp.dot(pack, rows_ref[...], preferred_element_type=F32)
    for z, out in enumerate(outs[:-1]):
        out[:, :width] = packed[z * block : (z + 1) * block].astype(BF16)
        back[z].start()
    for c in back:
        c.wait()


def split_kernel(cells, count, *refs):
    own_ref, oth_ref = refs[-2:]
    vals = [r[:, : own_ref.shape[1]].astype(F32) for r in refs[:count]]
    own_ref[...] = jnp.concatenate([v[:cells] for v in vals], axis=0).astype(BF16)
    oth_ref[...] = jnp.concatenate([v[cells:] for v in vals], axis=0).astype(BF16)


def join_kernel(count, *refs):
    refs[-1][...] = jnp.concatenate([r[...].astype(F32) for r in refs[:count]], axis=0).astype(BF16)


def half_kernel(keep_ref, core_ref, *refs):
    outs = refs[-4:]
    rows = outs[0].shape[0]
    for i, out in enumerate(outs):
        part = slice(i * rows, (i + 1) * rows)
        out[...] = (keep_ref[part, :] + core_ref[...].astype(F32)[part]).astype(out.dtype)


def lend_kernel(cells, keep_ref, core_ref, home_ref, *outs):
    total = keep_ref[...] + core_ref[...].astype(F32)
    rows = total.shape[0] // 4
    for i, out in enumerate((home_ref,) + outs):
        z, blocks = (0, range(4)) if i == 0 else ((i + 1) // 2, ((0, 1), (2, 3))[(i - 1) % 2])
        parts = [total[b * rows + z * cells : b * rows + (z + 1) * cells] for b in blocks]
        out[...] = jnp.concatenate(parts, axis=0).astype(out.dtype)


def regroup_kernel(cells, count, *refs):
    ins = [r[...].astype(F32) for r in refs[: 2 * count - 1]]
    vals = ins[:1] + [jnp.concatenate(ins[i : i + 2], axis=0) for i in range(1, 2 * count - 1, 2)]
    for b, out in enumerate(refs[-4:]):
        out[...] = jnp.concatenate([v[b * cells : (b + 1) * cells] for v in vals], axis=0).astype(out.dtype)


def weighted(weights, groups):
    rows = jnp.concatenate([g.astype(F32) for g in groups], axis=0).astype(BF16)
    return jnp.dot(weights.astype(BF16), rows, preferred_element_type=F32)


def gathered(cells, count, own_ref, x_ref, y_ref, d_ref):
    own = own_ref[...] + x_ref[...].astype(F32)
    oth = y_ref[...].astype(F32) + d_ref[...].astype(F32)
    parts = [slice(z * cells, (z + 1) * cells) for z in range(count)]
    return [jnp.concatenate([own[p], oth[p]], axis=0).astype(BF16) for p in parts]


def weigh_kernel(cells, count, own_ref, x_ref, y_ref, d_ref, *refs):
    wides, outs = refs[:count], refs[-count:]
    width, toks, block = own_ref.shape[1], outs[0].shape[0], 2 * cells
    left = []
    for z, wide in enumerate(wides):
        place = lax.broadcasted_iota(I32, (block, count * block), 1) - lax.broadcasted_iota(I32, (block, count * block), 0)
        shift = jnp.where(place == z * block, 1.0, 0.0).astype(BF16)
        left.append(across(wide[:, width:], shift)[: 3 * toks])
    val = weighted(jnp.concatenate(left, axis=0), gathered(cells, count, own_ref, x_ref, y_ref, d_ref))
    for z, out in enumerate(outs):
        a, b, c = (val[(3 * z + i) * toks : (3 * z + i + 1) * toks] for i in range(3))
        out[...] = (a + b + c).astype(out.dtype)


def combine_kernel(cells, count, own_ref, x_ref, y_ref, d_ref, table_ref, out_ref):
    toks = out_ref.shape[0]
    val = weighted(table_ref[...], gathered(cells, count, own_ref, x_ref, y_ref, d_ref))
    out_ref[...] = val[:toks] + val[toks : 2 * toks] + val[2 * toks :]


def finish_kernel(near_ref, top_ref, out_ref):
    out_ref[...] = (near_ref[...] + top_ref[...].astype(F32)).astype(BF16)


def fetch_kernel(count, *refs):
    ins, outs, sem = refs[:count], refs[-count - 1 : -1], refs[-1]
    copies = [pltpu.make_async_copy(a, b, sem.at[i]) for i, (a, b) in enumerate(zip(ins, outs))]
    for c in copies:
        c.start()
    for c in copies:
        c.wait()


def up_kernel(near, far, *refs):
    rows, (gate_ref, up_ref), (far_hid, near_hid, acc_g, acc_u) = refs[:4], refs[4:6], refs[6:]
    acc_g[...] = jnp.zeros_like(acc_g)
    acc_u[...] = jnp.zeros_like(acc_u)

    def part(at, wat, step):
        x = jnp.concatenate([r[:, pl.ds(at, step)] for r in rows], axis=0)
        acc_g[...] += jnp.dot(x, gate_ref[pl.ds(wat, step), :], preferred_element_type=F32)
        acc_u[...] += jnp.dot(x, up_ref[pl.ds(wat, step), :], preferred_element_type=F32)

    sweep(part, 0, rows[0].shape[1], acc_g.shape[0] <= 256)
    g = acc_g[...]
    hid = (g / (1.0 + jnp.exp(-g)) * acc_u[...]).astype(BF16)
    far_hid[...] = hid[:far]
    near_hid[...] = hid[far:]


def down_kernel(far_ref, near_ref, down_ref, *outs):
    hid = jnp.concatenate([far_ref[...], near_ref[...]], axis=0)
    rows = outs[0].shape[0]

    def part(at, wat, step):
        val = jnp.dot(hid, down_ref[:, pl.ds(wat, step)], preferred_element_type=F32)
        for i, out in enumerate(outs):
            out[:, pl.ds(at, step)] = val[i * rows : (i + 1) * rows].astype(out.dtype)

    sweep(part, 0, outs[0].shape[1], rows <= 128)


def per_device(
    hidden_in, expert_ids, gate_weights, replica_pick, placement, capacity, w_gate, w_up, w_down
):
    toks, width = hidden_in.shape
    top = expert_ids.shape[1]
    slots = placement.shape[0]
    devices = lax.axis_size("node")
    members = devices // slots
    cells = members * max(1, toks * top // (slots * members))
    high = slots // 2
    fw = w_gate.shape[1]
    my_slot = lax.axis_index("node") // members
    rows = high // 2 * cells
    any_ref = pl.BlockSpec(memory_space=pl.ANY)

    def send(value, flip):
        return lax.ppermute(value, "node", [(d, d ^ flip) for d in range(devices)])

    def over_z(block, z):
        return send(block, 2 * members * z)

    def split(blocks, when):
        return call(
            functools.partial(split_kernel, cells, len(blocks)),
            [shape((rows, width), BF16)] * 2,
            [VMEM] * len(blocks) + [any_ref] * len(when),
            "split",
        )(*blocks, *when)

    def fetch(arrays, when):
        return call(
            functools.partial(fetch_kernel, len(arrays)),
            [shape(w.shape, w.dtype) for w in arrays],
            [HBM] * len(arrays) + [any_ref] * len(when),
            "fetch",
            moved=sum(4 * w.size for w in arrays),
            limit=40,
            scratch=[pltpu.SemaphoreType.DMA((len(arrays),))],
        )(*arrays, *when)

    def spread(own, oth):
        d, y, x = send(oth, members + 2), send(oth, members), send(own, 2)
        return own, x, y, d

    def join(blocks, when):
        return call(
            functools.partial(join_kernel, 4),
            [shape((4 * rows, width), BF16)],
            [VMEM] * 4 + [any_ref] * len(when),
            "join",
        )(*blocks, *when)[0]

    half_z = high // 2
    block = 2 * cells
    lanes = -(-3 * toks // 128) * 128
    inputs = (expert_ids.T, gate_weights.T, replica_pick.T, placement[None, :], capacity[None, :], hidden_in)
    made = (
        [shape((block, width), BF16)] * half_z
        + [shape((block, width + lanes), BF16)] * half_z
        + [shape((3 * toks, half_z * block), F32)]
    )
    route = call(
        functools.partial(route_kernel, cells, half_z),
        made,
        [SMEM] + [HBM] * 6,
        "route",
        limit=60,
        scratch=[pltpu.VMEM(a.shape, a.dtype) for a in made]
        + [pltpu.VMEM(a.shape, a.dtype) for a in inputs]
        + [pltpu.SemaphoreType.DMA((6,)), pltpu.SemaphoreType.DMA((len(made),))],
        out=HBM,
    )(my_slot.reshape(1).astype(I32), *inputs)
    near_tab = route[-1]
    near_z = [over_z(route[z], z) for z in range(1, half_z)]
    far_wide = [over_z(route[z], z) for z in range(half_z, high)]
    (home,) = fetch([route[0]], ())
    near_own, near_oth = split([home] + near_z, ())
    near_got = spread(near_own, near_oth)
    (wg,) = fetch([w_gate], (near_own,))
    far_own, far_oth = split(far_wide, (wg,))
    far_got = spread(far_own, far_oth)
    near_all = join(near_got, (far_own,))
    near_core = send(near_all, 1)
    wu, wd = fetch([w_up, w_down], (near_all,))
    far_all = join(far_got, (wd,))
    far_core = send(far_all, 1)
    far_hid, near_hid, _, _ = call(
        functools.partial(up_kernel, 8 * rows, 8 * rows),
        [shape((8 * rows, fw), BF16)] * 2 + [shape((16 * rows, fw), F32)] * 2,
        [VMEM] * 6,
        "up",
        flops=64 * rows * fw * width,
    )(far_all, far_core, near_all, near_core, wg, wu)

    def half(keep, got, when):
        return call(
            half_kernel,
            [shape((rows, width), F32)] + [shape((rows, width), BF16)] * 3,
            [VMEM] * 2 + [any_ref] * len(when),
            "half",
        )(keep, got, *when)

    def gather(own, x, y, d):
        dg, yg, xg = send(d, members + 2), send(y, members), send(x, 2)
        return own, xg, yg, dg

    far_keep, far_give, near_keep, near_give = call(
        down_kernel,
        [shape((4 * rows, width), F32), shape((4 * rows, width), BF16)] * 2,
        [VMEM] * 3,
        "down",
        flops=32 * rows * fw * width,
    )(far_hid, near_hid, wd)
    far_sib = send(far_give, 1)
    near_sib = send(near_give, 1)
    far_half = half(far_keep, far_sib, ())
    lent = call(
        functools.partial(lend_kernel, cells),
        [shape((4 * cells, width), F32)] + [shape((2 * cells, width), BF16)] * (2 * half_z - 2),
        [VMEM] * 2,
        "lend",
    )(near_keep, near_sib)
    near_z = [lent[0]] + [over_z(lent[i], (i + 1) // 2) for i in range(1, 2 * half_z - 1)]
    far_sum = call(
        functools.partial(weigh_kernel, cells, half_z),
        [shape((toks, width), F32)] + [shape((toks, width), BF16)] * (half_z - 1),
        [VMEM] * (4 + half_z),
        "weigh",
    )(*gather(*far_half), *far_wide)
    near_half = call(
        functools.partial(regroup_kernel, cells, half_z),
        [shape((rows, width), F32)] + [shape((rows, width), BF16)] * 3,
        [VMEM] * (2 * half_z - 1) + [any_ref],
        "regroup",
    )(*near_z, far_sum[0])
    top_sum = far_sum[0]
    for z in range(1, half_z):
        top_sum = top_sum + over_z(far_sum[z], z).astype(F32)
    top_back = over_z(top_sum.astype(BF16), half_z)
    (near_part,) = call(
        functools.partial(combine_kernel, cells, half_z),
        [shape((toks, width), F32)],
        [VMEM] * 5,
        "combine",
    )(*gather(*near_half), near_tab)
    (mixed,) = call(finish_kernel, [shape((toks, width), BF16)], [VMEM] * 2, "finish")(near_part, top_back)
    return mixed


def solution(mesh):
    split = P(("grp", "node"), None)
    placed = (split, split, split, split, P(), P(), P(None, "node"), P(None, "node"), P("node", None))
    return jax.shard_map(per_device, mesh=mesh, in_specs=placed, out_specs=split, check_vma=False)
```
